256 devices in a mesh: tiles: 64 (over x, z_lo, y), dp: 4 (over z_hi, core).
Axes of the slice: x: 4, y: 4, z: 8 (z_hi: 2, z_lo: 4; z = z_hi * 4 + z_lo), core: 2. Of those that a mesh axis runs over, the one named last changes fastest.
Arguments:
- sea_state: bfloat16 [4, 64, 64, 64, 128], P('dp', 'tiles'), may hold values from -6 to 6
- cotangent: bfloat16 [4, 64, 64, 64, 128], P('dp', 'tiles'), may hold values from -6 to 6
- kernel: float32 [7, 7, 128], replicated, may hold values from -0.875 to 0.875
- conv_bias: float32 [128], replicated, may hold values from -4 to 4
- ln_gain: float32 [128], replicated, may hold values from 0.25 to 1.75
- ln_bias: float32 [128], replicated, may hold values from -3 to 3
- w_in: bfloat16 [128, 512], replicated, may hold values from -0.5 to 0.5
- b_in: float32 [512], replicated, may hold values from -3 to 3
- w_out: bfloat16 [512, 128], replicated, may hold values from -0.25 to 0.25
- b_out: float32 [128], replicated, may hold values from -3 to 3
- layer_scale: float32 [128], replicated, may hold values from 0.5 to 1.5
- tile_deal: int32 [64], replicated, may hold values from 0 to 63, each once
- adjacency: int32 [64, 8], replicated, may hold values from -1 to 63, as said below
Outputs:
- out_field: bfloat16 [4, 64, 64, 64, 128], P('dp', 'tiles')
- grad_field: bfloat16 [4, 64, 64, 64, 128], P('dp', 'tiles')
- grad_kernel: float32 [7, 7, 128], replicated
- grad_conv_bias: float32 [128], replicated
- grad_ln_gain: float32 [128], replicated
- grad_ln_bias: float32 [128], replicated
- grad_w_in: float32 [128, 512], replicated
- grad_b_in: float32 [512], replicated
- grad_w_out: float32 [512, 128], replicated
- grad_b_out: float32 [128], replicated
- grad_layer_scale: float32 [128], replicated
The draws below stay inside these ranges and needn't reach their ends.
Inputs may be any that keep to these rules, and one draw needn't show every extreme that they name: The window is 4 tile rows by 32 tile columns, of which 64 are wet, numbered in row order; neighbours wrap in longitude and not in latitude; adjacency is symmetric, and no two directions of one tile name the same tile.
All inputs are finite; a program needn't handle non-finite values.
Results may differ from the reference program's by a relative error of at most 0.0072.
Values may be sent and summed in bfloat16 or wider, within the bound.
A program may use at most 128 MiB of HBM per device.

```python
import math
import jax
import jax.numpy as jnp
from jax import lax

C = 128
HID = 512
TILE = 64
KERNEL = 7
LATS = 4
SNAPS = 4
TILES = 64


def draw_adjacency(key, part):
    key = jax.random.fold_in(key, 7)
    columns = TILES // 2
    cells = LATS * columns
    order = jax.random.permutation(key, cells - 2)
    wet_flag = jnp.concatenate([order < TILES - 2, jnp.ones((2,), dtype=bool)])
    ident = jnp.cumsum(wet_flag.astype(jnp.int32)) - 1
    ident = jnp.where(wet_flag, ident, -1).astype(jnp.int32)
    grid = ident.reshape(LATS, columns)
    padded = jnp.pad(grid, ((1, 1), (0, 0)), constant_values=-1)
    moves = ((-1, 0), (1, 0), (0, -1), (0, 1), (-1, -1), (-1, 1), (1, -1), (1, 1))
    looked = []
    for row_step, col_step in moves:
        rolled = jnp.roll(padded, -col_step, axis=1)
        looked.append(rolled[1 + row_step:1 + row_step + LATS])
    table = jnp.stack(looked, axis=-1).reshape(cells, 8)
    target = jnp.where(wet_flag, ident, TILES).astype(jnp.int32)
    result = jnp.full((TILES, 8), -1, jnp.int32)
    return result.at[target].set(table, mode='drop')


def block_scale(stream_key, shape, pieces, smallest, high):
    gain, own = 1.0, jax.random.fold_in(stream_key, 6)
    for axis_at, parts in pieces:
        heights = jnp.exp(jax.random.uniform(jax.random.fold_in(own, axis_at), (parts,), jnp.float32, smallest / len(pieces), high / len(pieces)))
        gain = gain * jnp.repeat(heights, shape[axis_at] // parts).reshape([-1 if axis == axis_at else 1 for axis in range(len(shape))])
    return gain


def bell_draw(key, shape, deviation, limit, cuts=(), kind=jnp.bfloat16):
    array = deviation * jax.random.normal(key, shape, jnp.float32)
    if cuts:
        array = array * block_scale(key, shape, cuts, -0.22, 0.18)
    return jnp.clip(array, -limit, limit).astype(kind)


def setup_inputs(seed: int = 0) -> dict:
    streams_of = jax.random.split(jax.random.key(seed), 14)
    sea_state = bell_draw(streams_of[0], (SNAPS, TILES, TILE, TILE, C), 1.0, 6.0, ((0, 4), (1, 64)))
    cotangent = bell_draw(streams_of[1], (SNAPS, TILES, TILE, TILE, C), 1.0, 6.0, ((0, 4), (1, 64)))
    kernel = bell_draw(streams_of[2], (KERNEL, KERNEL, C), (KERNEL * KERNEL) ** -0.5, 0.875, (), jnp.float32)
    conv_bias = bell_draw(streams_of[3], (C,), 1.0, 4.0, (), jnp.float32)
    ln_gain = jnp.clip(1.0 + 0.15 * jax.random.normal(streams_of[4], (C,), jnp.float32), 0.25, 1.75)
    ln_bias = bell_draw(streams_of[5], (C,), 0.5, 3.0, (), jnp.float32)
    w_in = bell_draw(streams_of[6], (C, HID), C ** -0.5, 0.5)
    b_in = bell_draw(streams_of[7], (HID,), 0.5, 3.0, (), jnp.float32)
    w_out = bell_draw(streams_of[8], (HID, C), HID ** -0.5, 0.25)
    b_out = bell_draw(streams_of[9], (C,), 0.5, 3.0, (), jnp.float32)
    layer_scale = jnp.clip(jax.random.uniform(streams_of[10], (C,), jnp.float32, 0.5, 1.5), 0.5, 1.5)
    tile_deal = jax.random.permutation(streams_of[11], TILES).astype(jnp.int32)
    adjacency = draw_adjacency(jax.random.fold_in(streams_of[13], 71), 0)
    return dict(sea_state=sea_state, cotangent=cotangent, kernel=kernel, conv_bias=conv_bias, ln_gain=ln_gain, ln_bias=ln_bias, w_in=w_in, b_in=b_in, w_out=w_out, b_out=b_out, layer_scale=layer_scale, tile_deal=tile_deal, adjacency=adjacency)


def frame_of(own_tile):
    return jnp.stack([own_tile[:, -3:], own_tile[:, :3], jnp.swapaxes(own_tile[:, :, -3:], 1, 2), jnp.swapaxes(own_tile[:, :, :3], 1, 2)])

def expand(frame):
    strip_len = frame.shape[-2]
    bottom = frame[..., 0, :, :, :, :]
    top_rows = frame[..., 1, :, :, :, :]

    def pad_corner(piece):
        return jnp.pad(piece, [(0, 0)] * (piece.ndim - 2) + [(0, strip_len - 3), (0, 0)])
    corners = [pad_corner(bottom[..., -3:, :]), pad_corner(bottom[..., :3, :]), pad_corner(top_rows[..., -3:, :]), pad_corner(top_rows[..., :3, :])]
    return jnp.concatenate([frame, jnp.stack(corners, axis=-5)], axis=-5)

def assemble(own_tile, halo_rows):
    west_cells = jnp.swapaxes(halo_rows[2], 1, 2)
    east_cells = jnp.swapaxes(halo_rows[3], 1, 2)
    middle = jnp.concatenate([west_cells, own_tile, east_cells], axis=2)
    upper_band = jnp.concatenate([halo_rows[4][:, :, :3], halo_rows[0], halo_rows[5][:, :, :3]], axis=2)
    lower_band = jnp.concatenate([halo_rows[6][:, :, :3], halo_rows[1], halo_rows[7][:, :, :3]], axis=2)
    return jnp.concatenate([upper_band, middle, lower_band], axis=1)

def depthwise(padded, kernel, tile_size, flipped):
    taps = kernel.shape[0]
    total = jnp.zeros(padded.shape[:1] + (tile_size, tile_size, padded.shape[-1]), jnp.float32)
    for i in range(taps):
        band = padded[:, i:i + tile_size]
        row_sum = None
        for j in range(taps):
            weight = kernel[taps - 1 - i, taps - 1 - j] if flipped else kernel[i, j]
            term = weight * band[:, :, j:j + tile_size].astype(jnp.float32)
            row_sum = term if row_sum is None else row_sum + term
        total = total + row_sum
    return total

def local_pass(own_tile, padded, upstream, kernel, conv_bias, ln_gain, ln_bias, w_in, b_in, w_out, b_out, layer_scale):
    tile_size = own_tile.shape[1]
    channels = own_tile.shape[-1]
    convolved = depthwise(padded, kernel, tile_size, False) + conv_bias
    row_mean = lax.optimization_barrier(jnp.mean(convolved, -1, keepdims=True))
    centred = convolved - row_mean
    inv_std = lax.rsqrt(lax.optimization_barrier(jnp.mean(centred * centred, -1, keepdims=True)) + 1e-06)
    whitened = centred * inv_std
    normed = (whitened * ln_gain + ln_bias).astype(jnp.bfloat16).reshape(-1, channels)
    pre_act = jnp.dot(normed, w_in, preferred_element_type=jnp.float32) + b_in
    act_full, gelu_back = jax.vjp(jax.nn.gelu, pre_act)
    activation = act_full.astype(jnp.bfloat16)
    branch_out = jnp.dot(activation, w_out, preferred_element_type=jnp.float32) + b_out
    flat_input = own_tile.reshape(-1, channels).astype(jnp.float32)
    result = (flat_input + layer_scale * branch_out).astype(jnp.bfloat16).reshape(own_tile.shape)
    up_rows = upstream.reshape(-1, channels).astype(jnp.float32)
    grad_out = up_rows * layer_scale
    grad_out16 = grad_out.astype(jnp.bfloat16)
    grad_scale = lax.optimization_barrier(jnp.sum(up_rows * branch_out, 0))
    grad_bout = lax.optimization_barrier(jnp.sum(grad_out, 0))
    grad_wout = jnp.dot(activation.T, grad_out16, preferred_element_type=jnp.float32)
    grad_act = jnp.dot(grad_out16, w_out.T, preferred_element_type=jnp.float32)
    grad_pre = gelu_back(grad_act)[0]
    grad_pre16 = grad_pre.astype(jnp.bfloat16)
    grad_bin = lax.optimization_barrier(jnp.sum(grad_pre, 0))
    grad_win = jnp.dot(normed.T, grad_pre16, preferred_element_type=jnp.float32)
    grad_normed = jnp.dot(grad_pre16, w_in.T, preferred_element_type=jnp.float32).reshape(whitened.shape)
    grad_gain = lax.optimization_barrier(jnp.sum(grad_normed * whitened, (0, 1, 2)))
    grad_lnb = lax.optimization_barrier(jnp.sum(grad_normed, (0, 1, 2)))
    grad_white = grad_normed * ln_gain
    grad_conv = inv_std * (grad_white - lax.optimization_barrier(jnp.mean(grad_white, -1, keepdims=True)) - whitened * lax.optimization_barrier(jnp.mean(grad_white * whitened, -1, keepdims=True)))
    grad_cbias = lax.optimization_barrier(jnp.sum(grad_conv, (0, 1, 2)))
    return (result, grad_conv.astype(jnp.bfloat16), (grad_cbias, grad_gain, grad_lnb, grad_win, grad_bin, grad_wout, grad_bout, grad_scale))

def second_pass(padded, padded_grad, grad_conv16, upstream, kernel):
    tile_size = upstream.shape[1]
    taps = kernel.shape[0]
    grad_input = (upstream.astype(jnp.float32) + depthwise(padded_grad, kernel, tile_size, True)).astype(jnp.bfloat16)
    rows_list = []
    for i in range(taps):
        for j in range(taps):
            rows_list.append(lax.optimization_barrier(jnp.sum(padded[:, i:i + tile_size, j:j + tile_size].astype(jnp.float32) * grad_conv16.astype(jnp.float32), (0, 1, 2))))
    return (grad_input, jnp.stack(rows_list).reshape(taps, taps, -1))

def reference(sea_state, cotangent, kernel, conv_bias, ln_gain, ln_bias, w_in, b_in, w_out, b_out, layer_scale, tile_deal, adjacency):
    holder = jnp.zeros((TILES,), jnp.int32).at[tile_deal].set(jnp.arange(TILES, dtype=jnp.int32))
    near_tiles = adjacency[tile_deal]
    is_wet = near_tiles >= 0
    source = holder[jnp.maximum(near_tiles, 0)]
    by_tile = jnp.swapaxes(sea_state, 0, 1)
    up_by_tile = jnp.swapaxes(cotangent, 0, 1)

    def halo_for(stacked):
        all_pieces = jax.vmap(lambda one: expand(frame_of(one)))(stacked)
        picked = all_pieces[source, jnp.arange(8, dtype=jnp.int32)[None, :]]
        return jnp.where(is_wet[:, :, None, None, None, None], picked, jnp.zeros((), stacked.dtype))
    input_halo = halo_for(by_tile)

    def first(items):
        own_tile, halo_rows, upstream = items
        padded = assemble(own_tile, halo_rows)
        return local_pass(own_tile, padded, upstream, kernel, conv_bias, ln_gain, ln_bias, w_in, b_in, w_out, b_out, layer_scale)
    results, grad_convs, grad_parts = lax.map(first, (by_tile, input_halo, up_by_tile))
    grad_halo = halo_for(grad_convs)

    def second(items):
        own_tile, halo_rows, grad_conv16, grad_rows, upstream = items
        return second_pass(assemble(own_tile, halo_rows), assemble(grad_conv16, grad_rows), grad_conv16, upstream, kernel)
    grad_inputs, kernel_parts = lax.map(second, (by_tile, input_halo, grad_convs, grad_halo, up_by_tile))
    factor = 1.0 / math.sqrt(SNAPS * TILES * TILE * TILE)
    sums = [lax.optimization_barrier(jnp.sum(part, 0)) * factor for part in grad_parts]
    grad_taps = lax.optimization_barrier(jnp.sum(kernel_parts, 0)) * factor
    return (jnp.swapaxes(results, 0, 1), jnp.swapaxes(grad_inputs, 0, 1), grad_taps, sums[0], sums[1], sums[2], sums[3], sums[4], sums[5], sums[6], sums[7])
```

```python
import functools
import math

import jax
import jax.numpy as jnp
from jax import lax
from jax.experimental import pallas as pl
from jax.experimental.pallas import tpu as pltpu
from jax.sharding import PartitionSpec as P

MESH = pl.DeviceIdType.MESH
F32 = jnp.float32
BF16 = jnp.bfloat16

T = 64
C = 128
HID = 512
NT = 64
PW = T + 6
NCH = 52
ROWS = 4
CELLS = ROWS * T
STEPS = T // ROWS
VMEM_LIMIT = 56 * 1024 * 1024

SUM_ROWS = 1040
TAP_ROWS = 56
ALL_ROWS = 1280
HALF = ALL_ROWS // 2
PIECE = HALF // 16
SCALE = 1.0 / math.sqrt(4 * NT * T * T)


def pack_natural(x_ref, frame, left, right, corner):
    for m in range(3):
        for a in range(4):
            frame[4 * m + a] = x_ref[T - 3 + m, pl.ds(16 * a, 16), :]
            frame[12 + 4 * m + a] = x_ref[m, pl.ds(16 * a, 16), :]
    left[...] = x_ref[:, 0:16, :].astype(F32).reshape(T * 16, C)
    right[...] = x_ref[:, T - 16 : T, :].astype(F32).reshape(T * 16, C)
    for c in range(3):
        for b in range(4):
            frame[24 + 4 * c + b] = right[pl.ds(256 * b + 13 + c, 16, stride=16), :].astype(BF16)
            frame[36 + 4 * c + b] = left[pl.ds(256 * b + c, 16, stride=16), :].astype(BF16)
    for n, (rows, cols, at) in enumerate(
        ((T - 3, right, 13), (T - 3, left, 0), (0, right, 13), (0, left, 0))
    ):
        corner[...] = jnp.zeros((16, C), F32)
        for r in range(3):
            corner[pl.ds(4 * r, 3), :] = cols[pl.ds((rows + r) * 16 + at, 3), :]
        frame[48 + n] = corner[...].astype(BF16)


def pack_dealt(g_ref, frame, left, right, corner):
    for m in range(3):
        for a in range(4):
            frame[4 * m + a] = g_ref[T - 3 + m, pl.ds(16 * a, 16), :]
            frame[12 + 4 * m + a] = g_ref[m, pl.ds(16 * a, 16), :]
    left[...] = g_ref[:, 0:32, :].astype(F32).reshape(T * 32, C)
    right[...] = g_ref[:, T - 32 : T, :].astype(F32).reshape(T * 32, C)
    for c in range(3):
        for b in range(4):
            frame[24 + 4 * c + b] = right[pl.ds(512 * b + 8 * c + 15, 16, stride=32), :].astype(BF16)
            frame[36 + 4 * c + b] = left[pl.ds(512 * b + 8 * c, 16, stride=32), :].astype(BF16)
    for n, (rows, cols, at) in enumerate(
        ((T - 3, right, 15), (T - 3, left, 0), (0, right, 15), (0, left, 0))
    ):
        corner[...] = jnp.zeros((16, C), F32)
        for r in range(3):
            for c in range(3):
                corner[pl.ds(4 * r + c, 1), :] = cols[pl.ds((rows + r) * 32 + at + 8 * c, 1), :]
        frame[48 + n] = corner[...].astype(BF16)


def wait_bytes(ref, count, sem):
    part = ref.at[pl.ds(0, count)]
    pltpu.make_async_copy(part, part, sem).wait()


def exchange_kernel(
    pack, src_ref, x_ref, halo_ref, frame, left, right, corner, held, chosen, send1, recv1, send2, recv2
):
    me = lax.axis_index("tiles")
    barrier = pltpu.get_barrier_semaphore()

    def greet(o, carry):
        pl.semaphore_signal(
            barrier, inc=1, device_id={"tiles": lax.rem(me + o, NT)}, device_id_type=MESH
        )
        return carry

    lax.fori_loop(1, NT, greet, 0)
    pack(x_ref, frame, left, right, corner)
    held[NT] = jnp.zeros((16, C), BF16)
    pl.semaphore_wait(barrier, NT - 1)

    def spread(o, carry):
        chunk = lax.rem(me + o, NT)

        @pl.when(chunk < NCH)
        def _():
            pltpu.make_async_remote_copy(
                src_ref=frame.at[chunk],
                dst_ref=held.at[me],
                send_sem=send1,
                recv_sem=recv1,
                device_id={"tiles": chunk},
                device_id_type=MESH,
            ).start()

        return carry

    lax.fori_loop(1, NT, spread, 0)

    @pl.when(me < NCH)
    def _():
        held[me] = frame[me]
        wait_bytes(held, NT - 1, recv1)

        def hand_on(o, carry):
            to = lax.rem(me + o, NT)
            chosen[to] = held[src_ref[to]]
            pltpu.make_async_remote_copy(
                src_ref=chosen.at[to],
                dst_ref=halo_ref.at[me],
                send_sem=send2,
                recv_sem=recv2,
                device_id={"tiles": to},
                device_id_type=MESH,
            ).start()
            return carry

        lax.fori_loop(1, NT, hand_on, 0)
        halo_ref[me] = held[src_ref[me]]
        wait_bytes(halo_ref, NCH - 1, recv2)
        wait_bytes(held, NCH - 1, send1)
        wait_bytes(held, NT - 1, send2)

    @pl.when(me >= NCH)
    def _():
        wait_bytes(halo_ref, NCH, recv2)
        wait_bytes(held, NCH, send1)


def exchange(x, src, dealt, collective_id):
    width = 32 if dealt else 16
    return pl.pallas_call(
        functools.partial(exchange_kernel, pack_dealt if dealt else pack_natural),
        out_shape=jax.ShapeDtypeStruct((NCH, 16, C), BF16),
        in_specs=[
            pl.BlockSpec(memory_space=pltpu.SMEM),
            pl.BlockSpec(memory_space=pltpu.VMEM),
        ],
        out_specs=pl.BlockSpec(memory_space=pltpu.VMEM),
        scratch_shapes=[
            pltpu.VMEM((NCH, 16, C), BF16),
            pltpu.VMEM((T * width, C), F32),
            pltpu.VMEM((T * width, C), F32),
            pltpu.VMEM((16, C), F32),
            pltpu.VMEM((NT + 1, 16, C), BF16),
            pltpu.VMEM((NT, 16, C), BF16),
            pltpu.SemaphoreType.DMA,
            pltpu.SemaphoreType.DMA,
            pltpu.SemaphoreType.DMA,
            pltpu.SemaphoreType.DMA,
        ],
        compiler_params=pltpu.CompilerParams(
            collective_id=collective_id, has_side_effects=True, vmem_limit_bytes=VMEM_LIMIT
        ),
        name="exchange_grad" if dealt else "exchange_input",
    )(src, x)


PITCH = 80
QROW = 14 * 8


def build_input(sea_ref, halo_ref, nat, corner, q_ref):
    def own(p, carry):
        at = pl.multiple_of((p + 3) * PITCH + 8, 8)
        nat[pl.ds(at, T), :] = sea_ref[p].astype(F32)
        return carry

    lax.fori_loop(0, T, own, 0)
    for m in range(3):
        for a in range(4):
            nat[pl.ds(m * PITCH + 8 + 16 * a, 16), :] = halo_ref[4 * m + a].astype(F32)
            nat[pl.ds((67 + m) * PITCH + 8 + 16 * a, 16), :] = halo_ref[12 + 4 * m + a].astype(F32)
    for c in range(3):
        for b in range(4):
            at = (3 + 16 * b) * PITCH
            nat[pl.ds(at + 5 + c, 16, stride=PITCH), :] = halo_ref[24 + 4 * c + b].astype(F32)
            nat[pl.ds(at + 72 + c, 16, stride=PITCH), :] = halo_ref[36 + 4 * c + b].astype(F32)
    for n, (row, at) in enumerate(((0, 5), (0, 72), (67, 5), (67, 72))):
        corner[...] = halo_ref[48 + n].astype(F32)
        for r in range(3):
            nat[pl.ds((row + r) * PITCH + at, 3), :] = corner[pl.ds(4 * r, 3), :]

    def deal(p, carry):
        for k in range(14):
            q_ref[p, pl.ds(8 * k, 8), :] = nat[pl.ds(p * PITCH + 5 + k, 8, stride=8), :]
        return carry

    lax.fori_loop(0, PW, deal, 0)


def conv_row(q_ref, taps, row, flipped):
    acc = None
    for i in range(7):
        x = q_ref[row + i].reshape(14, 8, C)
        for j in range(7):
            tap = taps[48 - 7 * i - j] if flipped else taps[7 * i + j]
            term = x[j : j + 8] * tap
            acc = term if acc is None else acc + term
    return acc


def spread_taps(k_ref, taps):
    for i in range(7):
        for j in range(7):
            taps[7 * i + j] = jnp.broadcast_to(k_ref[i, pl.ds(j, 1), :], (8, C))


def fold(x):
    return jnp.sum(x.reshape(x.shape[0] // 8, 8, x.shape[1]), 0)


def dot(a, b, contract):
    return lax.dot_general(a, b, (contract, ((), ())), preferred_element_type=F32)


def block_kernel(
    sea_ref,
    halo_ref,
    cot_ref,
    k_ref,
    cb_ref,
    gain_ref,
    lnb_ref,
    win_ref,
    bin_ref,
    wout_ref,
    bout_ref,
    ls_ref,
    out_ref,
    g_ref,
    q_ref,
    sums_ref,
    nat,
    corner,
    taps,
    conv,
    work,
    acc_win,
    acc_wout,
    acc_bin,
    acc_vec,
):
    step = pl.program_id(0)

    @pl.when(step == 0)
    def _():
        build_input(sea_ref, halo_ref, nat, corner, q_ref)
        spread_taps(k_ref, taps)
        acc_win[...] = jnp.zeros_like(acc_win)
        acc_wout[...] = jnp.zeros_like(acc_wout)
        acc_bin[...] = jnp.zeros_like(acc_bin)
        acc_vec[...] = jnp.zeros_like(acc_vec)

    first = step * ROWS

    def one_row(p, carry):
        conv[pl.ds(pl.multiple_of(p * T, T), T), :] = conv_row(q_ref, taps, first + p, False).reshape(T, C)
        return carry

    lax.fori_loop(0, ROWS, one_row, 0)

    work[...] = cot_ref[...].astype(F32).reshape(CELLS, C)
    up = jnp.concatenate(
        [work[pl.ds(p * T + k, 8, stride=8), :] for p in range(ROWS) for k in range(8)], 0
    )
    convolved = conv[...] + cb_ref[...]
    centred = convolved - jnp.mean(convolved, -1, keepdims=True)
    inv_std = lax.rsqrt(jnp.mean(centred * centred, -1, keepdims=True) + 1e-06)
    whitened = centred * inv_std
    normed = (whitened * gain_ref[...] + lnb_ref[...]).astype(BF16)
    grad_out = up * ls_ref[...]
    grad_out16 = grad_out.astype(BF16)

    branch = bout_ref[...]
    grad_normed = None
    width = 256
    c0 = math.sqrt(2 / math.pi)
    c1 = c0 * 0.044715
    for h in range(HID // width):
        hid = pl.ds(h * width, width)
        v = dot(normed, win_ref[:, hid], ((1,), (0,))) + bin_ref[:, hid]
        v2 = v * v
        t = jnp.tanh(v * (c0 + c1 * v2))
        half = 0.5 + 0.5 * t
        act = v * half
        slope = half + act * (1.0 - t) * (c0 + (3 * c1) * v2)
        act16 = act.astype(BF16)
        branch = branch + dot(act16, wout_ref[hid, :], ((1,), (0,)))
        acc_wout[:, hid] += dot(grad_out16, act16, ((0,), (0,)))
        grad_pre = slope * dot(grad_out16, wout_ref[hid, :], ((1,), (1,)))
        grad_pre16 = grad_pre.astype(BF16)
        acc_bin[:, hid] += fold(grad_pre)
        acc_win[:, hid] += dot(normed, grad_pre16, ((0,), (0,)))
        part = dot(grad_pre16, win_ref[:, hid], ((1,), (1,)))
        grad_normed = part if grad_normed is None else grad_normed + part

    grad_white = grad_normed * gain_ref[...]
    grad_conv = inv_std * (
        grad_white
        - jnp.mean(grad_white, -1, keepdims=True)
        - whitened * jnp.mean(grad_white * whitened, -1, keepdims=True)
    )
    g_ref[...] = grad_conv.astype(BF16).reshape(ROWS, T, C)
    acc_vec[0] += fold(grad_conv)
    acc_vec[1] += fold(grad_normed * whitened)
    acc_vec[2] += fold(grad_normed)
    acc_vec[3] += fold(grad_out)
    acc_vec[4] += fold(up * branch)

    scaled = branch * ls_ref[...]
    for p in range(ROWS):
        for k in range(8):
            at = p * T + 8 * k
            work[pl.ds(p * T + k, 8, stride=8), :] = scaled[at : at + 8]
    own = sea_ref[pl.ds(first, ROWS)].astype(F32)
    out_ref[...] = (own + work[...].reshape(ROWS, T, C)).astype(BF16)

    @pl.when(step == STEPS - 1)
    def _():
        for n in range(4):
            block = pl.ds(n * C, C)
            sums_ref[block, :] = acc_win[:, block]
            sums_ref[pl.ds(512 + n * C, C), :] = acc_wout[:, block].T
            sums_ref[pl.ds(1024 + n, 1), :] = jnp.sum(acc_bin[:, block], 0, keepdims=True)
        for n in range(5):
            sums_ref[pl.ds(1028 + n, 1), :] = jnp.sum(acc_vec[n], 0, keepdims=True)
        sums_ref[pl.ds(1033, SUM_ROWS - 1033), :] = jnp.zeros((SUM_ROWS - 1033, C), F32)


def whole(shape):
    return pl.BlockSpec(shape, lambda s: (0,) * len(shape))


def block(sea, halo, cot, kernel, conv_bias, ln_gain, ln_bias, w_in, b_in, w_out, b_out, layer_scale):
    rows = pl.BlockSpec((ROWS, T, C), lambda s: (s, 0, 0))
    return pl.pallas_call(
        block_kernel,
        grid=(STEPS,),
        out_shape=(
            jax.ShapeDtypeStruct((T, T, C), BF16),
            jax.ShapeDtypeStruct((T, T, C), BF16),
            jax.ShapeDtypeStruct((PW, QROW, C), F32),
            jax.ShapeDtypeStruct((SUM_ROWS, C), F32),
        ),
        in_specs=[
            whole((T, T, C)),
            whole((NCH, 16, C)),
            rows,
            whole((7, 7, C)),
            whole((1, C)),
            whole((1, C)),
            whole((1, C)),
            whole((C, HID)),
            whole((1, HID)),
            whole((HID, C)),
            whole((1, C)),
            whole((1, C)),
        ],
        out_specs=(rows, rows, whole((PW, QROW, C)), whole((SUM_ROWS, C))),
        scratch_shapes=[
            pltpu.VMEM((PW * PITCH, C), F32),
            pltpu.VMEM((16, C), F32),
            pltpu.VMEM((49, 8, C), F32),
            pltpu.VMEM((CELLS, C), F32),
            pltpu.VMEM((CELLS, C), F32),
            pltpu.VMEM((C, HID), F32),
            pltpu.VMEM((C, HID), F32),
            pltpu.VMEM((8, HID), F32),
            pltpu.VMEM((5, 8, C), F32),
        ],
        compiler_params=pltpu.CompilerParams(
            dimension_semantics=("arbitrary",), vmem_limit_bytes=VMEM_LIMIT
        ),
        name="block",
    )(
        sea,
        halo,
        cot,
        kernel,
        conv_bias.reshape(1, C),
        ln_gain.reshape(1, C),
        ln_bias.reshape(1, C),
        w_in,
        b_in.reshape(1, HID),
        w_out,
        b_out.reshape(1, C),
        layer_scale.reshape(1, C),
    )


def build_grad(g_ref, halo_ref, corner, qg):
    lane = lax.broadcasted_iota(jnp.int32, (8, C), 0)

    def put(row, g):
        qg[row, pl.ds(24, T), :] = g.reshape(T, C)
        for k in range(3):
            qg[row, pl.ds(8 * k, 8), :] = pltpu.roll(g[5 + k], 1, 0)
            qg[row, pl.ds(88 + 8 * k, 8), :] = pltpu.roll(g[k], 7, 0)

    def own(p, carry):
        put(p + 3, g_ref[p].astype(F32).reshape(8, 8, C))
        return carry

    lax.fori_loop(0, T, own, 0)
    for m in range(3):
        for row, base in ((m, 0), (67 + m, 12)):
            put(
                row,
                jnp.concatenate(
                    [halo_ref[base + 4 * m + a].astype(F32).reshape(2, 8, C) for a in range(4)], 0
                ),
            )
    for c in range(3):
        for b in range(4):
            corner[...] = halo_ref[24 + 4 * c + b].astype(F32)
            for r in range(16):
                qg[3 + 16 * b + r, pl.ds(8 * c, 1), :] = corner[pl.ds(r, 1), :]
            corner[...] = halo_ref[36 + 4 * c + b].astype(F32)
            for r in range(16):
                qg[3 + 16 * b + r, pl.ds(88 + 8 * c + 7, 1), :] = corner[pl.ds(r, 1), :]
    for n, (row, at) in enumerate(((0, 0), (0, 95), (67, 0), (67, 95))):
        corner[...] = halo_ref[48 + n].astype(F32)
        for r in range(3):
            for c in range(3):
                qg[row + r, pl.ds(at + 8 * c, 1), :] = corner[pl.ds(4 * r + c, 1), :]


def taps_kernel(g_ref, halo_ref, q_ref, cot_ref, k_ref, out_ref, tapsum_ref, corner, taps, qg, work, acc):
    step = pl.program_id(0)

    @pl.when(step == 0)
    def _():
        build_grad(g_ref, halo_ref, corner, qg)
        spread_taps(k_ref, taps)
        acc[...] = jnp.zeros_like(acc)

    first = step * ROWS

    def one_row(p, carry):
        row = first + p
        total = conv_row(qg, taps, row, True)
        at = p * T
        for k in range(8):
            work[pl.ds(at + k, 8, stride=8), :] = total[k]
        g = qg[row + 3, pl.ds(24, T), :].reshape(8, 8, C)
        for i in range(7):
            x = q_ref[row + i].reshape(14, 8, C)
            for j in range(7):
                acc[7 * i + j] += jnp.sum(x[j : j + 8] * g, 0)
        return carry

    lax.fori_loop(0, ROWS, one_row, 0)
    out_ref[...] = (cot_ref[...].astype(F32) + work[...].reshape(ROWS, T, C)).astype(BF16)

    @pl.when(step == STEPS - 1)
    def _():
        for n in range(49):
            tapsum_ref[pl.ds(n, 1), :] = jnp.sum(acc[n], 0, keepdims=True)
        tapsum_ref[pl.ds(49, TAP_ROWS - 49), :] = jnp.zeros((TAP_ROWS - 49, C), F32)


def tap_pass(g, halo, q, cot, kernel):
    rows = pl.BlockSpec((ROWS, T, C), lambda s: (s, 0, 0))
    return pl.pallas_call(
        taps_kernel,
        grid=(STEPS,),
        out_shape=(
            jax.ShapeDtypeStruct((T, T, C), BF16),
            jax.ShapeDtypeStruct((TAP_ROWS, C), F32),
        ),
        in_specs=[
            whole((T, T, C)),
            whole((NCH, 16, C)),
            whole((PW, QROW, C)),
            rows,
            whole((7, 7, C)),
        ],
        out_specs=(rows, whole((TAP_ROWS, C))),
        scratch_shapes=[
            pltpu.VMEM((16, C), F32),
            pltpu.VMEM((49, 8, C), F32),
            pltpu.VMEM((PW, QROW, C), F32),
            pltpu.VMEM((CELLS, C), F32),
            pltpu.VMEM((49, 8, C), F32),
        ],
        compiler_params=pltpu.CompilerParams(
            dimension_semantics=("arbitrary",), vmem_limit_bytes=VMEM_LIMIT
        ),
        name="taps",
    )(g, halo, q, cot, kernel)


def sum_kernel(
    sums_ref,
    tapsum_ref,
    total_ref,
    buf,
    other,
    pieces,
    part,
    line,
    sent,
    landed,
):
    t, d = lax.axis_index("tiles"), lax.axis_index("dp")
    x, zl, y = lax.div(t, 16), lax.rem(lax.div(t, 4), 4), lax.rem(t, 4)
    zh, core = lax.div(d, 2), lax.rem(d, 2)
    q, z = 4 * x + y, 4 * zh + zl

    def in_plane(o):
        there = lax.rem(q + o, 16)
        return there, {"tiles": 16 * lax.div(there, 4) + 4 * zl + lax.rem(there, 4), "dp": d}

    def in_line(o):
        there = lax.rem(z + o, 8)
        return {"tiles": 16 * x + 4 * lax.rem(there, 4) + y, "dp": 2 * lax.div(there, 4) + core}

    twin = {"tiles": t, "dp": 2 * zh + (1 - core)}

    def send(stage, src, dst, device):
        copy = pltpu.make_async_remote_copy(
            src_ref=src,
            dst_ref=dst,
            send_sem=sent.at[stage],
            recv_sem=landed.at[stage],
            device_id=device,
            device_id_type=MESH,
        )
        copy.start()
        return copy

    def each(count, do):
        def body(o, carry):
            do(o)
            return carry

        lax.fori_loop(1, count, body, 0)

    barrier = pltpu.get_barrier_semaphore()
    pl.semaphore_signal(barrier, inc=1, device_id=twin, device_id_type=MESH)
    each(16, lambda o: pl.semaphore_signal(barrier, inc=1, device_id=in_plane(o)[1], device_id_type=MESH))
    each(8, lambda o: pl.semaphore_signal(barrier, inc=1, device_id=in_line(o), device_id_type=MESH))
    buf[pl.ds(0, SUM_ROWS), :] = sums_ref[...]
    buf[pl.ds(SUM_ROWS, TAP_ROWS), :] = tapsum_ref[...]
    rest = SUM_ROWS + TAP_ROWS
    buf[pl.ds(rest, ALL_ROWS - rest), :] = jnp.zeros((ALL_ROWS - rest, C), F32)
    pl.semaphore_wait(barrier, 23)

    mine = pl.multiple_of(core * HALF, HALF)
    yours = pl.multiple_of((1 - core) * HALF, HALF)
    first = send(0, buf.at[pl.ds(yours, HALF), :], other, twin)
    first.wait()
    other[...] += buf[pl.ds(mine, HALF), :]

    def scatter(o):
        there, device = in_plane(o)
        at = pl.multiple_of(there * PIECE, PIECE)
        send(1, other.at[pl.ds(at, PIECE), :], pieces.at[q], device)

    each(16, scatter)
    here = pl.multiple_of(q * PIECE, PIECE)
    pieces[q] = other[pl.ds(here, PIECE), :]
    wait_bytes(pieces, 15, landed.at[1])
    part[...] = jnp.sum(pieces[...], 0)

    each(8, lambda o: send(2, part, line.at[z], in_line(o)) and None)
    line[z] = part[...]
    wait_bytes(line, 7, landed.at[2])
    mine_total = total_ref.at[pl.ds(mine, HALF), :]
    total_ref[pl.ds(pl.multiple_of(mine + here, 8), PIECE), :] = jnp.sum(line[...], 0) * SCALE

    def gather(o):
        spot = total_ref.at[pl.ds(pl.multiple_of(mine + here, 8), PIECE), :]
        send(3, spot, spot, in_plane(o)[1])

    each(16, gather)
    wait_bytes(pieces, 15, landed.at[3])
    last = send(4, mine_total, mine_total, twin)
    wait_bytes(pieces, 15, sent.at[1])
    wait_bytes(line, 7, sent.at[2])
    wait_bytes(pieces, 15, sent.at[3])
    last.wait()


def sum_all(sums, tapsum):
    return pl.pallas_call(
        sum_kernel,
        out_shape=jax.ShapeDtypeStruct((ALL_ROWS, C), F32),
        in_specs=[pl.BlockSpec(memory_space=pltpu.VMEM)] * 2,
        out_specs=pl.BlockSpec(memory_space=pltpu.VMEM),
        scratch_shapes=[
            pltpu.VMEM((ALL_ROWS, C), F32),
            pltpu.VMEM((HALF, C), F32),
            pltpu.VMEM((16, PIECE, C), F32),
            pltpu.VMEM((PIECE, C), F32),
            pltpu.VMEM((8, PIECE, C), F32),
            pltpu.SemaphoreType.DMA((5,)),
            pltpu.SemaphoreType.DMA((5,)),
        ],
        compiler_params=pltpu.CompilerParams(
            collective_id=3, has_side_effects=True, vmem_limit_bytes=VMEM_LIMIT
        ),
        name="sum_all",
    )(sums, tapsum)


def sources(tile_deal, adjacency):
    me = lax.axis_index("tiles")
    way = jnp.where(me < 48, lax.div(me, 12), lax.rem(me, 4) + 4)
    ids = jnp.arange(NT, dtype=jnp.int32)
    picked = jnp.sum(jnp.where(jnp.arange(8)[None, :] == way, adjacency, 0), 1)
    near = jnp.sum(jnp.where(tile_deal[:, None] == ids[None, :], picked[None, :], 0), 1)
    holder = jnp.sum(jnp.where(near[:, None] == tile_deal[None, :], ids[None, :], 0), 1)
    return jnp.where(near < 0, NT, holder).astype(jnp.int32)


def on_device(
    sea_state,
    cotangent,
    kernel,
    conv_bias,
    ln_gain,
    ln_bias,
    w_in,
    b_in,
    w_out,
    b_out,
    layer_scale,
    tile_deal,
    adjacency,
):
    sea, cot = sea_state[0, 0], cotangent[0, 0]
    src = sources(tile_deal, adjacency)
    halo = exchange(sea, src, False, 1)
    out, grad_conv, q, sums = block(
        sea, halo, cot, kernel, conv_bias, ln_gain, ln_bias, w_in, b_in, w_out, b_out, layer_scale
    )
    grad_halo = exchange(grad_conv, src, True, 2)
    grad_field, tapsum = tap_pass(grad_conv, grad_halo, q, cot, kernel)
    total = sum_all(sums, tapsum)
    return (
        out[None, None],
        grad_field[None, None],
        total[SUM_ROWS : SUM_ROWS + 49].reshape(7, 7, C),
        total[1028],
        total[1029],
        total[1030],
        total[:512].reshape(4, C, C).transpose(1, 0, 2).reshape(C, HID),
        total[1024:1028].reshape(HID),
        total[512:1024],
        total[1031],
        total[1032],
    )


def solution(mesh):
    field = P("dp", "tiles", None, None, None)
    return jax.shard_map(
        on_device,
        mesh=mesh,
        in_specs=(field, field) + (P(),) * 11,
        out_specs=(field, field) + (P(),) * 9,
        check_vma=False,
    )
```

```python
import functools
import math

import jax
import jax.numpy as jnp
from jax import lax
from jax.experimental import pallas as pl
from jax.experimental.pallas import tpu as pltpu
from jax.sharding import PartitionSpec as P

MESH = pl.DeviceIdType.MESH
F32 = jnp.float32
BF16 = jnp.bfloat16

T = 64
C = 128
HID = 512
NT = 64
PW = T + 6
NCH = 52
VMEM_LIMIT = 60 * 1024 * 1024

QROW = 14 * 8
WPOS = (6, 4, 2, 0, 1, 3, 5, 7)
WOF = tuple(WPOS.index(n) for n in range(8))
BLOCKS = (
    ((1, 7), (9, 15)),
    ((0, 1), (7, 9), (15, 24)),
    ((24, 36),),
    ((36, 48),),
    ((48, 64),),
)

ALL_ROWS = 1024
HALF = ALL_ROWS // 2
PIECE = HALF // 16
SMALL = 64
SCALE = 1.0 / math.sqrt(4 * NT * T * T)


def rows(start, size, stride=None):
    return pl.ds(start, size) if stride is None else pl.ds(start, size, stride=stride)


def aligned(at):
    return at if isinstance(at, int) else pl.multiple_of(at, 8)


def wait_bytes(ref, count, sem):
    part = ref.at[pl.ds(0, count)]
    pltpu.make_async_copy(part, part, sem).wait()


def loop(first, last, do):
    def body(n, carry):
        do(n)
        return carry

    lax.fori_loop(first, last, body, 0)


def margins(q, row):
    base = row * QROW
    lane = lax.rem(lax.broadcasted_iota(jnp.int32, (24, C), 0), 8)
    west = q[rows(base + 24 + 39, 24), :]
    q[rows(aligned(base), 24), :] = jnp.where(lane == 0, 0.0, west)
    east = q[rows(base + 25, 24), :]
    q[rows(aligned(base + 88), 24), :] = jnp.where(lane == 7, 0.0, east)


def pack(q, frame, corner):
    for m in range(3):
        for a in range(4):
            frame[4 * m + a] = q[rows((T + m) * QROW + 24 + 16 * a, 16), :].astype(BF16)
            frame[12 + 4 * m + a] = q[rows((3 + m) * QROW + 24 + 16 * a, 16), :].astype(BF16)
    for c in range(3):
        for b in range(4):
            base = (3 + 16 * b) * QROW + 24
            frame[24 + 4 * c + b] = q[rows(base + 8 * (5 + c) + 7, 16, QROW), :].astype(BF16)
            frame[36 + 4 * c + b] = q[rows(base + 8 * c, 16, QROW), :].astype(BF16)
    corner[...] = jnp.zeros((16, C), F32)
    for n, (row, at) in enumerate(((T, 47), (T, 0), (3, 47), (3, 0))):
        for r in range(3):
            for c in range(3):
                corner[rows(4 * r + c, 1), :] = q[rows((row + r) * QROW + 24 + at + 8 * c, 1), :]
        frame[48 + n] = corner[...].astype(BF16)


def put_sides(q, halo):
    for c in range(3):
        for b in range(4):
            base = (3 + 16 * b) * QROW
            q[rows(base + 8 * c, 16, QROW), :] = halo[24 + 4 * c + b].astype(F32)
            q[rows(base + 88 + 8 * c + 7, 16, QROW), :] = halo[36 + 4 * c + b].astype(F32)


def put_ends(q, halo, corner):
    for m in range(3):
        for row, first in ((m, 0), (67 + m, 12)):
            for a in range(4):
                q[rows(row * QROW + 24 + 16 * a, 16), :] = halo[first + 4 * m + a].astype(F32)
            margins(q, row)
    for n, (row, at) in enumerate(((0, 0), (0, 95), (67, 0), (67, 95))):
        corner[...] = halo[48 + n].astype(F32)
        for r in range(3):
            for c in range(3):
                q[rows((row + r) * QROW + at + 8 * c, 1), :] = corner[rows(4 * r + c, 1), :]


def tap_at(taps, i, j, flipped):
    return taps[48 - 7 * i - j] if flipped else taps[7 * i + j]


def convolve(q, taps, field, group, flipped):
    first = group * 8
    for w in range(0, 8, 2):
        acc = [None] * 8
        for m in range(14):
            x = q[rows(aligned((first + m) * QROW + 8 * w), 64), :].reshape(8, 8, C)
            for r in range(8):
                i = m - r
                if 0 <= i < 7:
                    for j in range(7):
                        term = x[j : j + 2] * tap_at(taps, i, j, flipped)
                        acc[r] = term if acc[r] is None else acc[r] + term
        for r in range(8):
            for n in range(2):
                field[rows(aligned(WPOS[w + n] * 512 + 8 * (first + r)), 8), :] = acc[r][n]


def add_sides(q, taps, field, group, flipped):
    first = group * 8
    for side in range(2):
        acc = [None] * 3
        for i in range(7):
            for c in range(3):
                at = 8 * c if side == 0 else 88 + 8 * c + 7
                x = q[rows((first + i) * QROW + at, 8, QROW), :]
                for e in range(3):
                    j = c - e if side == 0 else 6 + c - e
                    if 0 <= j < 7:
                        term = x * tap_at(taps, i, j, flipped)
                        acc[e] = term if acc[e] is None else acc[e] + term
        for e in range(3):
            w, s = (e, 0) if side == 0 else (5 + e, 7)
            spot = rows(WPOS[w] * 512 + first * 8 + s, 8, 8)
            field[spot, :] = field[spot, :] + acc[e]


def add_ends(q, taps, field, flipped):
    for e in range(3):
        for row, inputs in ((e, range(3 - e)), (61 + e, range(6 - e, 7))):
            acc = None
            for i in inputs:
                x = q[rows((row + i) * QROW, QROW), :].reshape(14, 8, C)
                for j in range(7):
                    term = x[j : j + 8] * tap_at(taps, i, j, flipped)
                    acc = term if acc is None else acc + term
            for w in range(8):
                spot = rows(WPOS[w] * 512 + 8 * row, 8)
                field[spot, :] = field[spot, :] + acc[w]


def neighbours_in(q, halo, corner, taps, field, flipped):
    put_sides(q, halo)
    loop(0, 8, lambda group: add_sides(q, taps, field, group, flipped))
    put_ends(q, halo, corner)
    add_ends(q, taps, field, flipped)


def tap_sums(q, qg, acc, p):
    g = qg[rows(aligned((p + 3) * QROW + 24), T), :].reshape(8, 8, C)
    for i in range(7):
        x = q[rows(aligned((p + i) * QROW), QROW), :].reshape(14, 8, C)
        for j in range(7):
            acc[7 * i + j] += jnp.sum(x[j : j + 8] * g, 0)


def fold(x):
    return jnp.sum(x.reshape(x.shape[0] // 8, 8, x.shape[1]), 0)


def dot(a, b, contract):
    return lax.dot_general(a, b, (contract, ((), ())), preferred_element_type=F32)


def pointwise(runs, field, up_field, weights, nat, qg, sums):
    cb_ref, gain_ref, lnb_ref, win_ref, bin_ref, wout_ref, bout_ref, ls_ref = weights
    acc_win, acc_wout, acc_bin, acc_vec = sums

    def take(ref):
        parts = [ref[rows(a * 64, (b - a) * 64), :] for a, b in runs]
        return parts[0] if len(parts) == 1 else jnp.concatenate(parts, 0)

    convolved = take(field) + cb_ref[...]
    up = take(up_field)
    centred = convolved - jnp.mean(convolved, -1, keepdims=True)
    inv_std = lax.rsqrt(jnp.mean(centred * centred, -1, keepdims=True) + 1e-06)
    whitened = centred * inv_std
    normed = (whitened * gain_ref[...] + lnb_ref[...]).astype(BF16)
    grad_out = up * ls_ref[...]
    grad_out16 = grad_out.astype(BF16)
    c0 = math.sqrt(2 / math.pi)
    c1 = c0 * 0.044715
    v = dot(normed, win_ref[...], ((1,), (0,))) + bin_ref[...]
    v2 = v * v
    t = jnp.tanh(v * (c0 + c1 * v2))
    half = 0.5 + 0.5 * t
    act = v * half
    slope = half + act * (1.0 - t) * (c0 + (3 * c1) * v2)
    act16 = act.astype(BF16)
    branch = bout_ref[...] + dot(act16, wout_ref[...], ((1,), (0,)))
    acc_wout[...] += dot(grad_out16, act16, ((0,), (0,)))
    grad_pre = slope * dot(grad_out16, wout_ref[...], ((1,), (1,)))
    grad_pre16 = grad_pre.astype(BF16)
    acc_bin[...] += fold(grad_pre)
    acc_win[...] += dot(normed, grad_pre16, ((0,), (0,)))
    grad_normed = dot(grad_pre16, win_ref[...], ((1,), (1,)))
    grad_white = grad_normed * gain_ref[...]
    grad_conv = inv_std * (
        grad_white
        - jnp.mean(grad_white, -1, keepdims=True)
        - whitened * jnp.mean(grad_white * whitened, -1, keepdims=True)
    )
    acc_vec[0] += fold(grad_conv)
    acc_vec[1] += fold(grad_normed * whitened)
    acc_vec[2] += fold(grad_normed)
    acc_vec[3] += fold(grad_out)
    acc_vec[4] += fold(up * branch)
    scaled = branch * ls_ref[...]
    rounded = grad_conv.astype(BF16).astype(F32)
    at = 0
    for a, b in runs:
        for n in range(8 * a, 8 * b):
            w, p = WOF[n // 64], n % 64
            nat[rows(p * T + w, 8, 8), :] = scaled[at : at + 8]
            qg[rows((p + 3) * QROW + 24 + 8 * w, 8), :] = rounded[at : at + 8]
            at += 8


def kernel_body(
    src_ref,
    sea_ref,
    cot_ref,
    k_ref,
    cb_ref,
    gain_ref,
    lnb_ref,
    win_ref,
    bin_ref,
    wout_ref,
    bout_ref,
    ls_ref,
    out_ref,
    gf_ref,
    gk_ref,
    gcb_ref,
    ggain_ref,
    glnb_ref,
    gwin_ref,
    gbin_ref,
    gwout_ref,
    gbout_ref,
    gls_ref,
    q,
    qg,
    field,
    up_field,
    nat,
    taps,
    corner,
    tap_acc,
    acc_win,
    acc_wout,
    acc_bin,
    acc_vec,
    frames,
    held_in,
    held_grad,
    chosen,
    halos,
    buf,
    other,
    pieces,
    part,
    line,
    total,
    small,
    small_other,
    small_line,
    small_part,
    small_plane,
    small_total,
    ex_sent,
    ex_landed,
    sent,
    landed,
):
    t, d = lax.axis_index("tiles"), lax.axis_index("dp")
    x, zl, y = lax.div(t, 16), lax.rem(lax.div(t, 4), 4), lax.rem(t, 4)
    zh, core = lax.div(d, 2), lax.rem(d, 2)
    plane, z = 4 * x + y, 4 * zh + zl

    def in_plane(o):
        there = lax.rem(plane + o, 16)
        return there, {"tiles": 16 * lax.div(there, 4) + 4 * zl + lax.rem(there, 4), "dp": d}

    def in_line(o):
        there = lax.rem(z + o, 8)
        return there, {"tiles": 16 * x + 4 * lax.rem(there, 4) + y, "dp": 2 * lax.div(there, 4) + core}

    def in_tiles(o):
        there = lax.rem(t + o, NT)
        return there, {"tiles": there, "dp": d}

    twin = {"tiles": t, "dp": 2 * zh + (1 - core)}

    def send(src, dst, send_sem, recv_sem, device):
        copy = pltpu.make_async_remote_copy(
            src_ref=src,
            dst_ref=dst,
            send_sem=send_sem,
            recv_sem=recv_sem,
            device_id=device,
            device_id_type=MESH,
        )
        copy.start()
        return copy

    barrier = pltpu.get_barrier_semaphore()

    def greet(device):
        pl.semaphore_signal(barrier, inc=1, device_id=device, device_id_type=MESH)

    loop(1, NT, lambda o: greet(in_tiles(o)[1]))
    greet(twin)
    loop(0, 4, lambda n: greet({"tiles": 16 * x + 4 * n + y, "dp": 2 * (1 - zh) + core}))

    held = (held_in, held_grad)

    def spread(n):
        def one(o):
            chunk, device = in_tiles(o)

            @pl.when(chunk < NCH)
            def _():
                send(frames.at[n, chunk], held[n].at[t], ex_sent.at[n, 0], ex_landed.at[n, 0], device)

        held[n][NT] = jnp.zeros((16, C), BF16)
        loop(1, NT, one)

    def hand_on(n):
        @pl.when(t < NCH)
        def _():
            held[n][t] = frames[n, t]
            wait_bytes(held[n], NT - 1, ex_landed.at[n, 0])

            def one(o):
                to, device = in_tiles(o)
                chosen[n, to] = held[n][src_ref[to]]
                send(chosen.at[n, to], halos.at[n, t], ex_sent.at[n, 1], ex_landed.at[n, 1], device)

            loop(1, NT, one)
            halos[n, t] = held[n][src_ref[t]]

    def collect(n):
        @pl.when(t < NCH)
        def _():
            wait_bytes(halos.at[n], NCH - 1, ex_landed.at[n, 1])
            wait_bytes(held[n], NCH - 1, ex_sent.at[n, 0])
            wait_bytes(held[n], NT - 1, ex_sent.at[n, 1])

        @pl.when(t >= NCH)
        def _():
            wait_bytes(halos.at[n], NCH, ex_landed.at[n, 1])
            wait_bytes(held[n], NCH, ex_sent.at[n, 0])

    def deal_input(p):
        nat[rows(aligned(p * T), T), :] = sea_ref[p].astype(F32)
        for w in range(8):
            q[rows(aligned((p + 3) * QROW + 24 + 8 * w), 8), :] = nat[rows(p * T + w, 8, 8), :]
        margins(q, p + 3)

    def no_rows(q):
        for first in (0, 67 * QROW):
            q[rows(first, 3 * QROW), :] = jnp.zeros((3 * QROW, C), F32)

    no_rows(q)
    no_rows(qg)
    loop(0, T, deal_input)
    pack(q, frames.at[0], corner)
    for i in range(7):
        for j in range(7):
            taps[7 * i + j] = jnp.broadcast_to(k_ref[i, pl.ds(j, 1), :], (8, C))
    pl.semaphore_wait(barrier, NT - 1 + 5)
    spread(0)

    def deal_cotangent(p):
        nat[rows(aligned(p * T), T), :] = cot_ref[p].astype(F32)
        for w in range(8):
            up_field[rows(aligned(WPOS[w] * 512 + 8 * p), 8), :] = nat[rows(p * T + w, 8, 8), :]

    loop(0, T, deal_cotangent)
    for acc in (acc_win, acc_wout, acc_bin, acc_vec, tap_acc):
        acc[...] = jnp.zeros_like(acc)
    loop(0, 8, lambda group: convolve(q, taps, field, group, False))
    hand_on(0)

    weights = (cb_ref, gain_ref, lnb_ref, win_ref, bin_ref, wout_ref, bout_ref, ls_ref)
    sums = (acc_win, acc_wout, acc_bin, acc_vec)
    pointwise(BLOCKS[0], field, up_field, weights, nat, qg, sums)
    collect(0)
    neighbours_in(q, halos.at[0], corner, taps, field, False)
    for runs in BLOCKS[1:]:
        pointwise(runs, field, up_field, weights, nat, qg, sums)

    for n in range(4):
        block = pl.ds(n * C, C)
        buf[block, :] = acc_win[:, block]
        buf[pl.ds(512 + n * C, C), :] = acc_wout[:, block].T
    mine = pl.multiple_of(core * HALF, HALF)
    yours = pl.multiple_of((1 - core) * HALF, HALF)
    to_twin = send(buf.at[pl.ds(yours, HALF)], other, sent.at[0], landed.at[0], twin)
    loop(3, 3 + T, lambda row: margins(qg, row))
    pack(qg, frames.at[1], corner)
    spread(1)

    loop(0, T // 2, lambda p: tap_sums(q, qg, tap_acc, p))

    to_twin.wait()
    other[...] = other[...] + buf[pl.ds(mine, HALF), :]

    def scatter(o):
        there, device = in_plane(o)
        at = pl.multiple_of(there * PIECE, PIECE)
        send(other.at[pl.ds(at, PIECE)], pieces.at[plane], sent.at[1], landed.at[1], device)

    loop(1, 16, scatter)
    here = pl.multiple_of(plane * PIECE, PIECE)
    pieces[plane] = other[pl.ds(here, PIECE), :]
    hand_on(1)

    loop(T // 2, T, lambda p: tap_sums(q, qg, tap_acc, p))
    for n in range(49):
        small[rows(n, 1), :] = jnp.sum(tap_acc[n], 0, keepdims=True)
    for n in range(4):
        small[rows(49 + n, 1), :] = jnp.sum(acc_bin[:, pl.ds(n * C, C)], 0, keepdims=True)
    for n in range(5):
        small[rows(53 + n, 1), :] = jnp.sum(acc_vec[n], 0, keepdims=True)
    small[rows(58, 6), :] = jnp.zeros((6, C), F32)
    small_to_twin = send(small, small_other, sent.at[5], landed.at[5], twin)

    loop(0, 4, lambda group: convolve(qg, taps, field, group, True))

    wait_bytes(pieces, 15, landed.at[1])
    part[...] = jnp.sum(pieces[...], 0)
    loop(1, 8, lambda o: send(part, line.at[z], sent.at[2], landed.at[2], in_line(o)[1]) and None)
    line[z] = part[...]

    small_to_twin.wait()
    small[...] = small[...] + small_other[...]

    def small_scatter(o):
        there, device = in_line(o)
        at = pl.multiple_of(there * 8, 8)
        send(small.at[pl.ds(at, 8)], small_line.at[z], sent.at[6], landed.at[6], device)

    loop(1, 8, small_scatter)
    my_small = pl.multiple_of(z * 8, 8)
    small_line[z] = small[pl.ds(my_small, 8), :]

    loop(4, 8, lambda group: convolve(qg, taps, field, group, True))

    wait_bytes(line, 7, landed.at[2])
    my_piece = pl.multiple_of(mine + here, PIECE)
    total[pl.ds(my_piece, PIECE), :] = jnp.sum(line[...], 0) * SCALE

    def gather(o):
        spot = total.at[pl.ds(my_piece, PIECE)]
        send(spot, spot, sent.at[3], landed.at[3], in_plane(o)[1])

    loop(1, 16, gather)

    wait_bytes(small_line, 7, landed.at[6])
    small_part[...] = jnp.sum(small_line[...], 0)
    loop(
        1,
        16,
        lambda o: send(small_part, small_plane.at[plane], sent.at[7], landed.at[7], in_plane(o)[1]) and None,
    )
    small_plane[plane] = small_part[...]

    collect(1)
    neighbours_in(qg, halos.at[1], corner, taps, field, True)

    wait_bytes(small_plane, 15, landed.at[7])
    small_total[pl.ds(my_small, 8), :] = jnp.sum(small_plane[...], 0) * SCALE

    def small_gather(o):
        spot = small_total.at[pl.ds(my_small, 8)]
        send(spot, spot, sent.at[8], landed.at[8], in_line(o)[1])

    loop(1, 8, small_gather)
    wait_bytes(pieces, 15, landed.at[3])
    half = total.at[pl.ds(mine, HALF)]
    last = send(half, half, sent.at[4], landed.at[4], twin)

    def write_out(p):
        at = aligned(p * T)
        out_ref[p] = (sea_ref[p].astype(F32) + nat[rows(at, T), :]).astype(BF16)
        for w in range(8):
            nat[rows(p * T + w, 8, 8), :] = field[rows(aligned(WPOS[w] * 512 + 8 * p), 8), :]
        gf_ref[p] = (cot_ref[p].astype(F32) + nat[rows(at, T), :]).astype(BF16)

    loop(0, T, write_out)

    wait_bytes(small_line, 7, landed.at[8])
    for i in range(7):
        gk_ref[i] = small_total[rows(7 * i, 7), :]
    for n in range(4):
        gbin_ref[:, pl.ds(n * C, C)] = small_total[rows(49 + n, 1), :]
    for n, ref in enumerate((gcb_ref, ggain_ref, glnb_ref, gbout_ref, gls_ref)):
        ref[...] = small_total[rows(53 + n, 1), :]
    last.wait()
    for n in range(4):
        block = pl.ds(n * C, C)
        gwin_ref[:, block] = total[block, :]
    gwout_ref[...] = total[pl.ds(512, 512), :]

    wait_bytes(pieces, 15, sent.at[1])
    wait_bytes(line, 7, sent.at[2])
    wait_bytes(pieces, 15, sent.at[3])
    wait_bytes(small_line, 7, sent.at[6])
    wait_bytes(small_plane, 15, sent.at[7])
    wait_bytes(small_line, 7, sent.at[8])


def whole_block(src, sea, cot, kernel, conv_bias, ln_gain, ln_bias, w_in, b_in, w_out, b_out, layer_scale):
    vmem = pl.BlockSpec(memory_space=pltpu.VMEM)
    vec = jax.ShapeDtypeStruct((1, C), F32)
    f32 = lambda *shape: pltpu.VMEM(shape, F32)
    bf16 = lambda *shape: pltpu.VMEM(shape, BF16)
    return pl.pallas_call(
        kernel_body,
        out_shape=(
            jax.ShapeDtypeStruct((T, T, C), BF16),
            jax.ShapeDtypeStruct((T, T, C), BF16),
            jax.ShapeDtypeStruct((7, 7, C), F32),
            vec,
            vec,
            vec,
            jax.ShapeDtypeStruct((C, HID), F32),
            jax.ShapeDtypeStruct((1, HID), F32),
            jax.ShapeDtypeStruct((HID, C), F32),
            vec,
            vec,
        ),
        in_specs=[pl.BlockSpec(memory_space=pltpu.SMEM)] + [vmem] * 11,
        out_specs=(vmem,) * 11,
        scratch_shapes=[
            f32(PW * QROW, C),
            f32(PW * QROW, C),
            f32(T * T, C),
            f32(T * T, C),
            f32(T * T, C),
            f32(49, 8, C),
            f32(16, C),
            f32(49, 8, C),
            f32(C, HID),
            f32(C, HID),
            f32(8, HID),
            f32(5, 8, C),
            bf16(2, NCH, 16, C),
            bf16(NT + 1, 16, C),
            bf16(NT + 1, 16, C),
            bf16(2, NT, 16, C),
            bf16(2, NCH, 16, C),
            f32(ALL_ROWS, C),
            f32(HALF, C),
            f32(16, PIECE, C),
            f32(PIECE, C),
            f32(8, PIECE, C),
            f32(ALL_ROWS, C),
            f32(SMALL, C),
            f32(SMALL, C),
            f32(8, 8, C),
            f32(8, C),
            f32(16, 8, C),
            f32(SMALL, C),
            pltpu.SemaphoreType.DMA((2, 2)),
            pltpu.SemaphoreType.DMA((2, 2)),
            pltpu.SemaphoreType.DMA((9,)),
            pltpu.SemaphoreType.DMA((9,)),
        ],
        compiler_params=pltpu.CompilerParams(
            collective_id=1, has_side_effects=True, vmem_limit_bytes=VMEM_LIMIT
        ),
        name="whole_block",
    )(
        src,
        sea,
        cot,
        kernel,
        conv_bias.reshape(1, C),
        ln_gain.reshape(1, C),
        ln_bias.reshape(1, C),
        w_in,
        b_in.reshape(1, HID),
        w_out,
        b_out.reshape(1, C),
        layer_scale.reshape(1, C),
    )


def sources(tile_deal, adjacency):
    me = lax.axis_index("tiles")
    way = jnp.where(me < 48, lax.div(me, 12), lax.rem(me, 4) + 4)
    ids = jnp.arange(NT, dtype=jnp.int32)
    picked = jnp.sum(jnp.where(jnp.arange(8)[None, :] == way, adjacency, 0), 1)
    near = jnp.sum(jnp.where(tile_deal[:, None] == ids[None, :], picked[None, :], 0), 1)
    holder = jnp.sum(jnp.where(near[:, None] == tile_deal[None, :], ids[None, :], 0), 1)
    return jnp.where(near < 0, NT, holder).astype(jnp.int32)


def on_device(
    sea_state,
    cotangent,
    kernel,
    conv_bias,
    ln_gain,
    ln_bias,
    w_in,
    b_in,
    w_out,
    b_out,
    layer_scale,
    tile_deal,
    adjacency,
):
    src = sources(tile_deal, adjacency)
    out, gf, gk, gcb, ggain, glnb, gwin, gbin, gwout, gbout, gls = whole_block(
        src,
        sea_state[0, 0],
        cotangent[0, 0],
        kernel,
        conv_bias,
        ln_gain,
        ln_bias,
        w_in,
        b_in,
        w_out,
        b_out,
        layer_scale,
    )
    return (
        out[None, None],
        gf[None, None],
        gk,
        gcb.reshape(C),
        ggain.reshape(C),
        glnb.reshape(C),
        gwin,
        gbin.reshape(HID),
        gwout,
        gbout.reshape(C),
        gls.reshape(C),
    )


def solution(mesh):
    field = P("dp", "tiles", None, None, None)
    return jax.shard_map(
        on_device,
        mesh=mesh,
        in_specs=(field, field) + (P(),) * 11,
        out_specs=(field, field) + (P(),) * 9,
        check_vma=False,
    )
```

```python
import functools
import math

import jax
import jax.numpy as jnp
from jax import lax
from jax.experimental import pallas as pl
from jax.experimental.pallas import tpu as pltpu
from jax.sharding import PartitionSpec as P

MESH = pl.DeviceIdType.MESH
F32 = jnp.float32
BF16 = jnp.bfloat16

T = 64
C = 128
HID = 512
NT = 64
PW = T + 6
NCH = 52
VMEM_LIMIT = 60 * 1024 * 1024

QROW = 14 * 8
WPOS = (6, 4, 2, 0, 1, 3, 5, 7)
EDGE_ROWS = (0, 1, 2, 61, 62, 63)
EDGE_COLS = ((0, 0), (1, 0), (2, 0), (5, 7), (6, 7), (7, 7))
BORDER = 768
BLOCK = 1024

ALL_ROWS = 1024
HALF = ALL_ROWS // 2
PIECE = HALF // 16
SMALL = 64
SCALE = 1.0 / math.sqrt(4 * NT * T * T)


def rows(start, size, stride=None):
    return pl.ds(start, size) if stride is None else pl.ds(start, size, stride=stride)


def aligned(at):
    return at if isinstance(at, int) else pl.multiple_of(at, 8)


def wait_bytes(ref, count, sem):
    part = ref.at[pl.ds(0, count)]
    pltpu.make_async_copy(part, part, sem).wait()


def loop(first, last, do):
    def body(n, carry):
        do(n)
        return carry

    lax.fori_loop(first, last, body, 0)


def margins(q, row):
    base = row * QROW
    lane = lax.rem(lax.broadcasted_iota(jnp.int32, (24, C), 0), 8)
    west = q[rows(base + 24 + 39, 24), :]
    q[rows(aligned(base), 24), :] = jnp.where(lane == 0, 0.0, west)
    east = q[rows(base + 25, 24), :]
    q[rows(aligned(base + 88), 24), :] = jnp.where(lane == 7, 0.0, east)


def pack(q, frame, corner):
    for m in range(3):
        for a in range(4):
            frame[4 * m + a] = q[rows((T + m) * QROW + 24 + 16 * a, 16), :].astype(BF16)
            frame[12 + 4 * m + a] = q[rows((3 + m) * QROW + 24 + 16 * a, 16), :].astype(BF16)
    for c in range(3):
        for b in range(4):
            base = (3 + 16 * b) * QROW + 24
            frame[24 + 4 * c + b] = q[rows(base + 8 * (5 + c) + 7, 16, QROW), :].astype(BF16)
            frame[36 + 4 * c + b] = q[rows(base + 8 * c, 16, QROW), :].astype(BF16)
    corner[...] = jnp.zeros((16, C), F32)
    for n, (row, at) in enumerate(((T, 47), (T, 0), (3, 47), (3, 0))):
        for r in range(3):
            for c in range(3):
                corner[rows(4 * r + c, 1), :] = q[rows((row + r) * QROW + 24 + at + 8 * c, 1), :]
        frame[48 + n] = corner[...].astype(BF16)


def put_sides(q, halo):
    for c in range(3):
        for b in range(4):
            base = (3 + 16 * b) * QROW
            q[rows(base + 8 * c, 16, QROW), :] = halo[24 + 4 * c + b].astype(F32)
            q[rows(base + 88 + 8 * c + 7, 16, QROW), :] = halo[36 + 4 * c + b].astype(F32)


def put_ends(q, halo, corner):
    for m in range(3):
        for row, first in ((m, 0), (67 + m, 12)):
            for a in range(4):
                q[rows(row * QROW + 24 + 16 * a, 16), :] = halo[first + 4 * m + a].astype(F32)
            margins(q, row)
    for n, (row, at) in enumerate(((0, 0), (0, 95), (67, 0), (67, 95))):
        corner[...] = halo[48 + n].astype(F32)
        for r in range(3):
            for c in range(3):
                q[rows((row + r) * QROW + at + 8 * c, 1), :] = corner[rows(4 * r + c, 1), :]


def tap_at(taps, i, j, flipped):
    return taps[48 - 7 * i - j] if flipped else taps[7 * i + j]


def convolve(q, taps, field, group, flipped):
    first = group * 8
    for w in range(0, 8, 2):
        acc = [None] * 8
        for m in range(14):
            x = q[rows(aligned((first + m) * QROW + 8 * w), 64), :].reshape(8, 8, C)
            for r in range(8):
                i = m - r
                if 0 <= i < 7:
                    for j in range(7):
                        term = x[j : j + 2] * tap_at(taps, i, j, flipped)
                        acc[r] = term if acc[r] is None else acc[r] + term
        for r in range(8):
            for n in range(2):
                field[rows(aligned(WPOS[w + n] * 512 + 8 * (first + r)), 8), :] = acc[r][n]


def add_sides(q, taps, field, group, flipped):
    first = group * 8
    for side in range(2):
        acc = [None] * 3
        for i in range(7):
            for c in range(3):
                at = 8 * c if side == 0 else 88 + 8 * c + 7
                x = q[rows((first + i) * QROW + at, 8, QROW), :]
                for e in range(3):
                    j = c - e if side == 0 else 6 + c - e
                    if 0 <= j < 7:
                        term = x * tap_at(taps, i, j, flipped)
                        acc[e] = term if acc[e] is None else acc[e] + term
        for e in range(3):
            w, s = (e, 0) if side == 0 else (5 + e, 7)
            spot = rows(WPOS[w] * 512 + first * 8 + s, 8, 8)
            field[spot, :] = field[spot, :] + acc[e]


def add_ends(q, taps, field, flipped):
    for e in range(3):
        for row, inputs in ((e, range(3 - e)), (61 + e, range(6 - e, 7))):
            acc = None
            for i in inputs:
                x = q[rows((row + i) * QROW, QROW), :].reshape(14, 8, C)
                for j in range(7):
                    term = x[j : j + 8] * tap_at(taps, i, j, flipped)
                    acc = term if acc is None else acc + term
            for w in range(8):
                spot = rows(WPOS[w] * 512 + 8 * row, 8)
                field[spot, :] = field[spot, :] + acc[w]


def neighbours_in(q, halo, corner, taps, field, flipped):
    put_sides(q, halo)
    loop(0, 8, lambda group: add_sides(q, taps, field, group, flipped))
    put_ends(q, halo, corner)
    add_ends(q, taps, field, flipped)


def tap_sums(q, qg, acc, p):
    g = qg[rows(aligned((p + 3) * QROW + 24), T), :].reshape(8, 8, C)
    for i in range(7):
        x = q[rows(aligned((p + i) * QROW), QROW), :].reshape(14, 8, C)
        for j in range(7):
            acc[7 * i + j] += jnp.sum(x[j : j + 8] * g, 0)


def fold(x):
    return jnp.sum(x.reshape(x.shape[0] // 8, 8, x.shape[1]), 0)


def dot(a, b, contract):
    return lax.dot_general(a, b, (contract, ((), ())), preferred_element_type=F32)


def pointwise(convolved, up, weights, sums):
    cb_ref, gain_ref, lnb_ref, win_ref, bin_ref, wout_ref, bout_ref, ls_ref = weights
    acc_win, acc_wout, acc_bin, acc_vec = sums
    convolved = convolved + cb_ref[...]
    centred = convolved - jnp.mean(convolved, -1, keepdims=True)
    inv_std = lax.rsqrt(jnp.mean(centred * centred, -1, keepdims=True) + 1e-06)
    whitened = centred * inv_std
    normed = (whitened * gain_ref[...] + lnb_ref[...]).astype(BF16)
    grad_out = up * ls_ref[...]
    grad_out16 = grad_out.astype(BF16)
    c0 = math.sqrt(2 / math.pi)
    c1 = c0 * 0.044715
    v = dot(normed, win_ref[...], ((1,), (0,))) + bin_ref[...]
    v2 = v * v
    t = jnp.tanh(v * (c0 + c1 * v2))
    half = 0.5 + 0.5 * t
    act = v * half
    slope = half + act * (1.0 - t) * (c0 + (3 * c1) * v2)
    act16 = act.astype(BF16)
    branch = bout_ref[...] + dot(act16, wout_ref[...], ((1,), (0,)))
    acc_wout[...] += dot(grad_out16, act16, ((0,), (0,)))
    grad_pre = slope * dot(grad_out16, wout_ref[...], ((1,), (1,)))
    grad_pre16 = grad_pre.astype(BF16)
    acc_bin[...] += fold(grad_pre)
    acc_win[...] += dot(normed, grad_pre16, ((0,), (0,)))
    grad_normed = dot(grad_pre16, win_ref[...], ((1,), (1,)))
    grad_white = grad_normed * gain_ref[...]
    grad_conv = inv_std * (
        grad_white
        - jnp.mean(grad_white, -1, keepdims=True)
        - whitened * jnp.mean(grad_white * whitened, -1, keepdims=True)
    )
    acc_vec[0] += fold(grad_conv)
    acc_vec[1] += fold(grad_normed * whitened)
    acc_vec[2] += fold(grad_normed)
    acc_vec[3] += fold(grad_out)
    acc_vec[4] += fold(up * branch)
    return branch * ls_ref[...], grad_conv.astype(BF16).astype(F32)


def tile_block(b, field, up_field, weights, sums, nat, qg):
    spot = rows(pl.multiple_of(b * BLOCK, BLOCK), BLOCK)
    scaled, rounded = pointwise(field[spot, :], up_field[spot, :], weights, sums)
    for n, w in enumerate((3 - b, 4 + b)):
        for p in range(T):
            at = 512 * n + 8 * p
            nat[rows(p * T + w, 8, 8), :] = scaled[at : at + 8]
            qg[rows(aligned((p + 3) * QROW + 24 + 8 * w), 8), :] = rounded[at : at + 8]


def border_block(field, border_up, weights, sums, nat, qg):
    parts = [field[rows(WPOS[w] * 512 + 8 * p, 8), :] for p in EDGE_ROWS for w in range(8)]
    parts += [field[rows(WPOS[w] * 512 + 64 * n + s, 8, 8), :] for w, s in EDGE_COLS for n in range(8)]
    scaled, rounded = pointwise(jnp.concatenate(parts, 0), border_up[...], weights, sums)
    for e, (w, s) in enumerate(EDGE_COLS):
        for n in range(8):
            at = 384 + 64 * e + 8 * n
            nat[rows(8 * n * T + 8 * s + w, 8, T), :] = scaled[at : at + 8]
            qg[rows((8 * n + 3) * QROW + 24 + 8 * w + s, 8, QROW), :] = rounded[at : at + 8]
    for e, p in enumerate(EDGE_ROWS):
        for w in range(8):
            at = 64 * e + 8 * w
            nat[rows(p * T + w, 8, 8), :] = scaled[at : at + 8]
            qg[rows((p + 3) * QROW + 24 + 8 * w, 8), :] = rounded[at : at + 8]


def kernel_body(
    src_ref,
    sea_ref,
    cot_ref,
    k_ref,
    cb_ref,
    gain_ref,
    lnb_ref,
    win_ref,
    bin_ref,
    wout_ref,
    bout_ref,
    ls_ref,
    out_ref,
    gf_ref,
    gk_ref,
    gcb_ref,
    ggain_ref,
    glnb_ref,
    gwin_ref,
    gbin_ref,
    gwout_ref,
    gbout_ref,
    gls_ref,
    q,
    qg,
    field,
    up_field,
    border_up,
    nat,
    taps,
    corner,
    tap_acc,
    acc_win,
    acc_wout,
    acc_bin,
    acc_vec,
    frames,
    held_in,
    held_grad,
    chosen,
    halos,
    buf,
    other,
    pieces,
    part,
    line,
    total,
    small,
    small_other,
    small_line,
    small_part,
    small_plane,
    small_total,
    ex_sent,
    ex_landed,
    sent,
    landed,
):
    t, d = lax.axis_index("tiles"), lax.axis_index("dp")
    x, zl, y = lax.div(t, 16), lax.rem(lax.div(t, 4), 4), lax.rem(t, 4)
    zh, core = lax.div(d, 2), lax.rem(d, 2)
    plane, z = 4 * x + y, 4 * zh + zl

    def in_plane(o):
        there = lax.rem(plane + o, 16)
        return there, {"tiles": 16 * lax.div(there, 4) + 4 * zl + lax.rem(there, 4), "dp": d}

    def in_line(o):
        there = lax.rem(z + o, 8)
        return there, {"tiles": 16 * x + 4 * lax.rem(there, 4) + y, "dp": 2 * lax.div(there, 4) + core}

    def in_tiles(o):
        there = lax.rem(t + o, NT)
        return there, {"tiles": there, "dp": d}

    twin = {"tiles": t, "dp": 2 * zh + (1 - core)}

    def send(src, dst, send_sem, recv_sem, device):
        copy = pltpu.make_async_remote_copy(
            src_ref=src,
            dst_ref=dst,
            send_sem=send_sem,
            recv_sem=recv_sem,
            device_id=device,
            device_id_type=MESH,
        )
        copy.start()
        return copy

    barrier = pltpu.get_barrier_semaphore()

    def greet(device):
        pl.semaphore_signal(barrier, inc=1, device_id=device, device_id_type=MESH)

    loop(1, NT, lambda o: greet(in_tiles(o)[1]))
    greet(twin)
    loop(0, 4, lambda n: greet({"tiles": 16 * x + 4 * n + y, "dp": 2 * (1 - zh) + core}))

    held = (held_in, held_grad)

    def spread(n):
        def one(o):
            chunk, device = in_tiles(o)

            @pl.when(chunk < NCH)
            def _():
                send(frames.at[n, chunk], held[n].at[t], ex_sent.at[n, 0], ex_landed.at[n, 0], device)

        held[n][NT] = jnp.zeros((16, C), BF16)
        loop(1, NT, one)

    def hand_on(n):
        @pl.when(t < NCH)
        def _():
            held[n][t] = frames[n, t]
            wait_bytes(held[n], NT - 1, ex_landed.at[n, 0])

            def one(o):
                to, device = in_tiles(o)
                chosen[n, to] = held[n][src_ref[to]]
                send(chosen.at[n, to], halos.at[n, t], ex_sent.at[n, 1], ex_landed.at[n, 1], device)

            loop(1, NT, one)
            halos[n, t] = held[n][src_ref[t]]

    def collect(n):
        @pl.when(t < NCH)
        def _():
            wait_bytes(halos.at[n], NCH - 1, ex_landed.at[n, 1])
            wait_bytes(held[n], NCH - 1, ex_sent.at[n, 0])
            wait_bytes(held[n], NT - 1, ex_sent.at[n, 1])

        @pl.when(t >= NCH)
        def _():
            wait_bytes(halos.at[n], NCH, ex_landed.at[n, 1])
            wait_bytes(held[n], NCH, ex_sent.at[n, 0])

    def deal_input(p):
        nat[rows(aligned(p * T), T), :] = sea_ref[p].astype(F32)
        for w in range(8):
            q[rows(aligned((p + 3) * QROW + 24 + 8 * w), 8), :] = nat[rows(p * T + w, 8, 8), :]
        margins(q, p + 3)

    def no_rows(q):
        for first in (0, 67 * QROW):
            q[rows(first, 3 * QROW), :] = jnp.zeros((3 * QROW, C), F32)

    no_rows(q)
    no_rows(qg)
    loop(0, T, deal_input)
    pack(q, frames.at[0], corner)
    for i in range(7):
        for j in range(7):
            taps[7 * i + j] = jnp.broadcast_to(k_ref[i, pl.ds(j, 1), :], (8, C))
    pl.semaphore_wait(barrier, NT - 1 + 5)
    spread(0)

    lane = lax.broadcasted_iota(jnp.int32, (8, C), 0)

    def deal_cotangent(p):
        nat[rows(aligned(p * T), T), :] = cot_ref[p].astype(F32)
        for w in range(8):
            cells = nat[rows(p * T + w, 8, 8), :]
            if w < 3:
                cells = jnp.where(lane == 0, 0.0, cells)
            if w > 4:
                cells = jnp.where(lane == 7, 0.0, cells)
            up_field[rows(aligned(WPOS[w] * 512 + 8 * p), 8), :] = cells

    loop(0, T, deal_cotangent)
    for w in range(8):
        for first in (0, 61):
            up_field[rows(WPOS[w] * 512 + 8 * first, 24), :] = jnp.zeros((24, C), F32)
    for e, p in enumerate(EDGE_ROWS):
        for w in range(8):
            border_up[rows(64 * e + 8 * w, 8), :] = nat[rows(p * T + w, 8, 8), :]
    for e, (w, s) in enumerate(EDGE_COLS):
        for n in range(8):
            cells = nat[rows(8 * n * T + 8 * s + w, 8, T), :]
            if n == 0:
                cells = jnp.where(lane < 3, 0.0, cells)
            if n == 7:
                cells = jnp.where(lane > 4, 0.0, cells)
            border_up[rows(384 + 64 * e + 8 * n, 8), :] = cells
    for acc in (acc_win, acc_wout, acc_bin, acc_vec, tap_acc):
        acc[...] = jnp.zeros_like(acc)
    loop(0, 8, lambda group: convolve(q, taps, field, group, False))
    hand_on(0)

    weights = (cb_ref, gain_ref, lnb_ref, win_ref, bin_ref, wout_ref, bout_ref, ls_ref)
    sums = (acc_win, acc_wout, acc_bin, acc_vec)
    loop(0, 4, lambda b: tile_block(b, field, up_field, weights, sums, nat, qg))
    collect(0)
    neighbours_in(q, halos.at[0], corner, taps, field, False)
    border_block(field, border_up, weights, sums, nat, qg)

    for n in range(4):
        block = pl.ds(n * C, C)
        buf[block, :] = acc_win[:, block]
        buf[pl.ds(512 + n * C, C), :] = acc_wout[:, block].T
    mine = pl.multiple_of(core * HALF, HALF)
    yours = pl.multiple_of((1 - core) * HALF, HALF)
    to_twin = send(buf.at[pl.ds(yours, HALF)], other, sent.at[0], landed.at[0], twin)
    pack(qg, frames.at[1], corner)
    spread(1)
    loop(3, 3 + T, lambda row: margins(qg, row))

    def tap_rows(first, last):
        loop(first, last, lambda p: tap_sums(q, qg, tap_acc, p))

    def back_rows(first, last):
        loop(first, last, lambda group: convolve(qg, taps, field, group, True))

    tap_rows(0, 16)

    to_twin.wait()
    other[...] = other[...] + buf[pl.ds(mine, HALF), :]

    def scatter(o):
        there, device = in_plane(o)
        at = pl.multiple_of(there * PIECE, PIECE)
        send(other.at[pl.ds(at, PIECE)], pieces.at[plane], sent.at[1], landed.at[1], device)

    loop(1, 16, scatter)
    here = pl.multiple_of(plane * PIECE, PIECE)
    pieces[plane] = other[pl.ds(here, PIECE), :]

    tap_rows(16, T)
    for n in range(49):
        small[rows(n, 1), :] = jnp.sum(tap_acc[n], 0, keepdims=True)
    for n in range(4):
        small[rows(49 + n, 1), :] = jnp.sum(acc_bin[:, pl.ds(n * C, C)], 0, keepdims=True)
    for n in range(5):
        small[rows(53 + n, 1), :] = jnp.sum(acc_vec[n], 0, keepdims=True)
    small[rows(58, 6), :] = jnp.zeros((6, C), F32)
    small_to_twin = send(small, small_other, sent.at[5], landed.at[5], twin)
    hand_on(1)

    back_rows(0, 1)

    wait_bytes(pieces, 15, landed.at[1])
    part[...] = jnp.sum(pieces[...], 0)
    loop(1, 8, lambda o: send(part, line.at[z], sent.at[2], landed.at[2], in_line(o)[1]) and None)
    line[z] = part[...]

    small_to_twin.wait()
    small[...] = small[...] + small_other[...]

    def small_scatter(o):
        there, device = in_line(o)
        at = pl.multiple_of(there * 8, 8)
        send(small.at[pl.ds(at, 8)], small_line.at[z], sent.at[6], landed.at[6], device)

    loop(1, 8, small_scatter)
    my_small = pl.multiple_of(z * 8, 8)
    small_line[z] = small[pl.ds(my_small, 8), :]

    back_rows(1, 5)

    wait_bytes(small_line, 7, landed.at[6])
    small_part[...] = jnp.sum(small_line[...], 0)
    loop(
        1,
        16,
        lambda o: send(small_part, small_plane.at[plane], sent.at[7], landed.at[7], in_plane(o)[1]) and None,
    )
    small_plane[plane] = small_part[...]

    back_rows(5, 6)

    wait_bytes(line, 7, landed.at[2])
    my_piece = pl.multiple_of(mine + here, PIECE)
    total[pl.ds(my_piece, PIECE), :] = (jnp.sum(line[...], 0) * SCALE).astype(BF16)

    def gather(o):
        spot = total.at[pl.ds(my_piece, PIECE)]
        send(spot, spot, sent.at[3], landed.at[3], in_plane(o)[1])

    loop(1, 16, gather)

    back_rows(6, 8)

    wait_bytes(small_plane, 15, landed.at[7])
    small_total[pl.ds(my_small, 8), :] = jnp.sum(small_plane[...], 0) * SCALE

    def small_gather(o):
        spot = small_total.at[pl.ds(my_small, 8)]
        send(spot, spot, sent.at[8], landed.at[8], in_line(o)[1])

    loop(1, 8, small_gather)

    def write_out(p):
        at = aligned(p * T)
        out_ref[p] = (sea_ref[p].astype(F32) + nat[rows(at, T), :]).astype(BF16)

    loop(0, T, write_out)

    gathered = total.at[pl.ds(0, 15 * PIECE)]
    pltpu.make_async_copy(gathered, gathered, landed.at[3]).wait()
    half = total.at[pl.ds(mine, HALF)]
    last = send(half, half, sent.at[4], landed.at[4], twin)

    collect(1)
    neighbours_in(qg, halos.at[1], corner, taps, field, True)

    def write_grad(p):
        for w in range(8):
            nat[rows(p * T + w, 8, 8), :] = field[rows(aligned(WPOS[w] * 512 + 8 * p), 8), :]
        gf_ref[p] = (cot_ref[p].astype(F32) + nat[rows(aligned(p * T), T), :]).astype(BF16)

    loop(0, T, write_grad)

    wait_bytes(small_line, 7, landed.at[8])
    for i in range(7):
        gk_ref[i] = small_total[rows(7 * i, 7), :]
    for n in range(4):
        gbin_ref[:, pl.ds(n * C, C)] = small_total[rows(49 + n, 1), :]
    for n, ref in enumerate((gcb_ref, ggain_ref, glnb_ref, gbout_ref, gls_ref)):
        ref[...] = small_total[rows(53 + n, 1), :]
    last.wait()
    for n in range(4):
        block = pl.ds(n * C, C)
        gwin_ref[:, block] = total[block, :].astype(F32)
    gwout_ref[...] = total[pl.ds(512, 512), :].astype(F32)

    wait_bytes(pieces, 15, sent.at[1])
    wait_bytes(line, 7, sent.at[2])
    pltpu.make_async_copy(gathered, gathered, sent.at[3]).wait()
    wait_bytes(small_line, 7, sent.at[6])
    wait_bytes(small_plane, 15, sent.at[7])
    wait_bytes(small_line, 7, sent.at[8])


def whole_block(src, sea, cot, kernel, conv_bias, ln_gain, ln_bias, w_in, b_in, w_out, b_out, layer_scale):
    vmem = pl.BlockSpec(memory_space=pltpu.VMEM)
    vec = jax.ShapeDtypeStruct((1, C), F32)
    f32 = lambda *shape: pltpu.VMEM(shape, F32)
    bf16 = lambda *shape: pltpu.VMEM(shape, BF16)
    return pl.pallas_call(
        kernel_body,
        out_shape=(
            jax.ShapeDtypeStruct((T, T, C), BF16),
            jax.ShapeDtypeStruct((T, T, C), BF16),
            jax.ShapeDtypeStruct((7, 7, C), F32),
            vec,
            vec,
            vec,
            jax.ShapeDtypeStruct((C, HID), F32),
            jax.ShapeDtypeStruct((1, HID), F32),
            jax.ShapeDtypeStruct((HID, C), F32),
            vec,
            vec,
        ),
        in_specs=[pl.BlockSpec(memory_space=pltpu.SMEM)] + [vmem] * 11,
        out_specs=(vmem,) * 11,
        scratch_shapes=[
            f32(PW * QROW, C),
            f32(PW * QROW, C),
            f32(T * T, C),
            f32(T * T, C),
            f32(BORDER, C),
            f32(T * T, C),
            f32(49, 8, C),
            f32(16, C),
            f32(49, 8, C),
            f32(C, HID),
            f32(C, HID),
            f32(8, HID),
            f32(5, 8, C),
            bf16(2, NCH, 16, C),
            bf16(NT + 1, 16, C),
            bf16(NT + 1, 16, C),
            bf16(2, NT, 16, C),
            bf16(2, NCH, 16, C),
            f32(ALL_ROWS, C),
            f32(HALF, C),
            f32(16, PIECE, C),
            f32(PIECE, C),
            f32(8, PIECE, C),
            bf16(ALL_ROWS, C),
            f32(SMALL, C),
            f32(SMALL, C),
            f32(8, 8, C),
            f32(8, C),
            f32(16, 8, C),
            f32(SMALL, C),
            pltpu.SemaphoreType.DMA((2, 2)),
            pltpu.SemaphoreType.DMA((2, 2)),
            pltpu.SemaphoreType.DMA((9,)),
            pltpu.SemaphoreType.DMA((9,)),
        ],
        compiler_params=pltpu.CompilerParams(
            collective_id=1, has_side_effects=True, vmem_limit_bytes=VMEM_LIMIT
        ),
        name="whole_block",
    )(
        src,
        sea,
        cot,
        kernel,
        conv_bias.reshape(1, C),
        ln_gain.reshape(1, C),
        ln_bias.reshape(1, C),
        w_in,
        b_in.reshape(1, HID),
        w_out,
        b_out.reshape(1, C),
        layer_scale.reshape(1, C),
    )


HAND_ROWS = 16


def hand_over_kernel(*refs):
    count = (len(refs) - 2) // 3
    here, there = refs[-2:]
    parts = []
    for n in range(count):
        a, b, mid = refs[n], refs[count + n], refs[2 * count + n]
        if a.shape[0] == T:
            for first in range(0, T, HAND_ROWS):
                parts.append([r.at[pl.ds(first, HAND_ROWS)] for r in (a, mid, b)])
        else:
            parts.append([a, mid, b])
    arrive = [pltpu.make_async_copy(a, mid, here.at[n]) for n, (a, mid, _) in enumerate(parts)]
    leave = [pltpu.make_async_copy(mid, b, there.at[n]) for n, (_, mid, b) in enumerate(parts)]
    for copy in arrive:
        copy.start()
    for first, then in zip(arrive, leave):
        first.wait()
        then.start()
    for copy in leave:
        copy.wait()


def hand_over(*arrays):
    anywhere = pl.BlockSpec(memory_space=pl.ANY)
    parts = len(arrays) + sum(T // HAND_ROWS - 1 for a in arrays if a.shape[0] == T)
    return pl.pallas_call(
        hand_over_kernel,
        out_shape=tuple(jax.ShapeDtypeStruct(a.shape, a.dtype) for a in arrays),
        in_specs=[anywhere] * len(arrays),
        out_specs=(anywhere,) * len(arrays),
        scratch_shapes=[pltpu.VMEM(a.shape, a.dtype) for a in arrays]
        + [pltpu.SemaphoreType.DMA((parts,)), pltpu.SemaphoreType.DMA((parts,))],
        name="hand_over",
    )(*arrays)


def sources(tile_deal, adjacency):
    me = lax.axis_index("tiles")
    way = jnp.where(me < 48, lax.div(me, 12), lax.rem(me, 4) + 4)
    ids = jnp.arange(NT, dtype=jnp.int32)
    picked = jnp.sum(jnp.where(jnp.arange(8)[None, :] == way, adjacency, 0), 1)
    near = jnp.sum(jnp.where(tile_deal[:, None] == ids[None, :], picked[None, :], 0), 1)
    holder = jnp.sum(jnp.where(near[:, None] == tile_deal[None, :], ids[None, :], 0), 1)
    return jnp.where(near < 0, NT, holder).astype(jnp.int32)


def on_device(
    sea_state,
    cotangent,
    kernel,
    conv_bias,
    ln_gain,
    ln_bias,
    w_in,
    b_in,
    w_out,
    b_out,
    layer_scale,
    tile_deal,
    adjacency,
):
    src = sources(tile_deal, adjacency)
    out, gf, gk, gcb, ggain, glnb, gwin, gbin, gwout, gbout, gls = whole_block(
        src,
        sea_state[0, 0],
        cotangent[0, 0],
        kernel,
        conv_bias,
        ln_gain,
        ln_bias,
        w_in,
        b_in,
        w_out,
        b_out,
        layer_scale,
    )
    out, gf, gk, gcb, ggain, glnb, gwin, gbin, gwout, gbout, gls = hand_over(
        out, gf, gk, gcb, ggain, glnb, gwin, gbin, gwout, gbout, gls
    )
    return (
        out[None, None],
        gf[None, None],
        gk,
        gcb.reshape(C),
        ggain.reshape(C),
        glnb.reshape(C),
        gwin,
        gbin.reshape(HID),
        gwout,
        gbout.reshape(C),
        gls.reshape(C),
    )


def solution(mesh):
    field = P("dp", "tiles", None, None, None)
    return jax.shard_map(
        on_device,
        mesh=mesh,
        in_specs=(field, field) + (P(),) * 11,
        out_specs=(field, field) + (P(),) * 9,
        check_vma=False,
    )
```

```python
import functools
import math

import jax
import jax.numpy as jnp
from jax import lax
from jax.experimental import pallas as pl
from jax.experimental.pallas import tpu as pltpu
from jax.sharding import PartitionSpec as P

MESH = pl.DeviceIdType.MESH
F32 = jnp.float32
BF16 = jnp.bfloat16

T = 64
C = 128
HID = 512
NT = 64
PW = T + 6
NCH = 52
VMEM_LIMIT = 60 * 1024 * 1024

QROW = 14 * 8
WPOS = (6, 4, 2, 0, 1, 3, 5, 7)
EDGE_ROWS = (0, 1, 2, 61, 62, 63)
EDGE_COLS = ((0, 0), (1, 0), (2, 0), (5, 7), (6, 7), (7, 7))
BORDER = 768
BLOCK = 1024

ALL_ROWS = 1024
HALF = ALL_ROWS // 2
PIECE = HALF // 16
SMALL = 64
SCALE = 1.0 / math.sqrt(4 * NT * T * T)


def rows(start, size, stride=None):
    return pl.ds(start, size) if stride is None else pl.ds(start, size, stride=stride)


def aligned(at):
    return at if isinstance(at, int) else pl.multiple_of(at, 8)


def wait_bytes(ref, count, sem):
    part = ref.at[pl.ds(0, count)]
    pltpu.make_async_copy(part, part, sem).wait()


def loop(first, last, do):
    def body(n, carry):
        do(n)
        return carry

    lax.fori_loop(first, last, body, 0)


def margins(q, row):
    base = row * QROW
    lane = lax.rem(lax.broadcasted_iota(jnp.int32, (24, C), 0), 8)
    west = q[rows(base + 24 + 39, 24), :]
    q[rows(aligned(base), 24), :] = jnp.where(lane == 0, 0.0, west)
    east = q[rows(base + 25, 24), :]
    q[rows(aligned(base + 88), 24), :] = jnp.where(lane == 7, 0.0, east)


def pack(q, frame, corner):
    for m in range(3):
        for a in range(4):
            frame[4 * m + a] = q[rows((T + m) * QROW + 24 + 16 * a, 16), :].astype(BF16)
            frame[12 + 4 * m + a] = q[rows((3 + m) * QROW + 24 + 16 * a, 16), :].astype(BF16)
    for c in range(3):
        for b in range(4):
            base = (3 + 16 * b) * QROW + 24
            frame[24 + 4 * c + b] = q[rows(base + 8 * (5 + c) + 7, 16, QROW), :].astype(BF16)
            frame[36 + 4 * c + b] = q[rows(base + 8 * c, 16, QROW), :].astype(BF16)
    corner[...] = jnp.zeros((16, C), F32)
    for n, (row, at) in enumerate(((T, 47), (T, 0), (3, 47), (3, 0))):
        for r in range(3):
            for c in range(3):
                corner[rows(4 * r + c, 1), :] = q[rows((row + r) * QROW + 24 + at + 8 * c, 1), :]
        frame[48 + n] = corner[...].astype(BF16)


def put_sides(q, halo):
    for c in range(3):
        for b in range(4):
            base = (3 + 16 * b) * QROW
            q[rows(base + 8 * c, 16, QROW), :] = halo[24 + 4 * c + b].astype(F32)
            q[rows(base + 88 + 8 * c + 7, 16, QROW), :] = halo[36 + 4 * c + b].astype(F32)


def put_ends(q, halo, corner):
    for m in range(3):
        for row, first in ((m, 0), (67 + m, 12)):
            for a in range(4):
                q[rows(row * QROW + 24 + 16 * a, 16), :] = halo[first + 4 * m + a].astype(F32)
            margins(q, row)
    for n, (row, at) in enumerate(((0, 0), (0, 95), (67, 0), (67, 95))):
        corner[...] = halo[48 + n].astype(F32)
        for r in range(3):
            for c in range(3):
                q[rows((row + r) * QROW + at + 8 * c, 1), :] = corner[rows(4 * r + c, 1), :]


def tap_at(taps, i, j, flipped):
    return taps[48 - 7 * i - j] if flipped else taps[7 * i + j]


def convolve(q, taps, field, group, flipped):
    first = group * 8
    for w in range(0, 8, 2):
        acc = [None] * 8
        for m in range(14):
            x = q[rows(aligned((first + m) * QROW + 8 * w), 64), :].reshape(8, 8, C)
            for r in range(8):
                i = m - r
                if 0 <= i < 7:
                    for j in range(7):
                        term = x[j : j + 2] * tap_at(taps, i, j, flipped)
                        acc[r] = term if acc[r] is None else acc[r] + term
        for r in range(8):
            for n in range(2):
                field[rows(aligned(WPOS[w + n] * 512 + 8 * (first + r)), 8), :] = acc[r][n]


def add_sides(q, taps, field, group, flipped):
    first = group * 8
    for side in range(2):
        acc = [None] * 3
        for i in range(7):
            for c in range(3):
                at = 8 * c if side == 0 else 88 + 8 * c + 7
                x = q[rows((first + i) * QROW + at, 8, QROW), :]
                for e in range(3):
                    j = c - e if side == 0 else 6 + c - e
                    if 0 <= j < 7:
                        term = x * tap_at(taps, i, j, flipped)
                        acc[e] = term if acc[e] is None else acc[e] + term
        for e in range(3):
            w, s = (e, 0) if side == 0 else (5 + e, 7)
            spot = rows(WPOS[w] * 512 + first * 8 + s, 8, 8)
            field[spot, :] = field[spot, :] + acc[e]


def add_ends(q, taps, field, flipped):
    for e in range(3):
        for row, inputs in ((e, range(3 - e)), (61 + e, range(6 - e, 7))):
            acc = None
            for i in inputs:
                x = q[rows((row + i) * QROW, QROW), :].reshape(14, 8, C)
                for j in range(7):
                    term = x[j : j + 8] * tap_at(taps, i, j, flipped)
                    acc = term if acc is None else acc + term
            for w in range(8):
                spot = rows(WPOS[w] * 512 + 8 * row, 8)
                field[spot, :] = field[spot, :] + acc[w]


def neighbours_in(q, halo, corner, taps, field, flipped):
    put_sides(q, halo)
    loop(0, 8, lambda group: add_sides(q, taps, field, group, flipped))
    put_ends(q, halo, corner)
    add_ends(q, taps, field, flipped)


def tap_sums(q, qg, acc, p):
    g = qg[rows(aligned((p + 3) * QROW + 24), T), :].reshape(8, 8, C)
    for i in range(7):
        x = q[rows(aligned((p + i) * QROW), QROW), :].reshape(14, 8, C)
        for j in range(7):
            acc[7 * i + j] += jnp.sum(x[j : j + 8] * g, 0)


def fold(x):
    return jnp.sum(x.reshape(x.shape[0] // 8, 8, x.shape[1]), 0)


def dot(a, b, contract):
    return lax.dot_general(a, b, (contract, ((), ())), preferred_element_type=F32)


def pointwise(convolved, up, weights, sums):
    cb_ref, gain_ref, lnb_ref, win_ref, bin_ref, wout_ref, bout_ref, ls_ref = weights
    acc_win, acc_wout, acc_bin, acc_vec = sums
    convolved = convolved + cb_ref[...]
    centred = convolved - jnp.mean(convolved, -1, keepdims=True)
    inv_std = lax.rsqrt(jnp.mean(centred * centred, -1, keepdims=True) + 1e-06)
    whitened = centred * inv_std
    normed = (whitened * gain_ref[...] + lnb_ref[...]).astype(BF16)
    grad_out = up * ls_ref[...]
    grad_out16 = grad_out.astype(BF16)
    c0 = math.sqrt(2 / math.pi)
    c1 = c0 * 0.044715
    v = dot(normed, win_ref[...], ((1,), (0,))) + bin_ref[...]
    v2 = v * v
    t = jnp.tanh(v * (c0 + c1 * v2))
    half = 0.5 + 0.5 * t
    act = v * half
    slope = half + act * (1.0 - t) * (c0 + (3 * c1) * v2)
    act16 = act.astype(BF16)
    branch = bout_ref[...] + dot(act16, wout_ref[...], ((1,), (0,)))
    acc_wout[...] += dot(grad_out16, act16, ((0,), (0,)))
    grad_pre = slope * dot(grad_out16, wout_ref[...], ((1,), (1,)))
    grad_pre16 = grad_pre.astype(BF16)
    acc_bin[...] += fold(grad_pre)
    acc_win[...] += dot(normed, grad_pre16, ((0,), (0,)))
    grad_normed = dot(grad_pre16, win_ref[...], ((1,), (1,)))
    grad_white = grad_normed * gain_ref[...]
    grad_conv = inv_std * (
        grad_white
        - jnp.mean(grad_white, -1, keepdims=True)
        - whitened * jnp.mean(grad_white * whitened, -1, keepdims=True)
    )
    acc_vec[0] += fold(grad_conv)
    acc_vec[1] += fold(grad_normed * whitened)
    acc_vec[2] += fold(grad_normed)
    acc_vec[3] += fold(grad_out)
    acc_vec[4] += fold(up * branch)
    return branch * ls_ref[...], grad_conv.astype(BF16).astype(F32)


def tile_block(b, field, up_field, weights, sums, nat, qg):
    spot = rows(pl.multiple_of(b * BLOCK, BLOCK), BLOCK)
    scaled, rounded = pointwise(field[spot, :], up_field[spot, :], weights, sums)
    for n, w in enumerate((3 - b, 4 + b)):
        for p in range(T):
            at = 512 * n + 8 * p
            nat[rows(p * T + w, 8, 8), :] = scaled[at : at + 8]
            qg[rows(aligned((p + 3) * QROW + 24 + 8 * w), 8), :] = rounded[at : at + 8]


def border_block(field, border_up, weights, sums, nat, qg):
    parts = [field[rows(WPOS[w] * 512 + 8 * p, 8), :] for p in EDGE_ROWS for w in range(8)]
    parts += [field[rows(WPOS[w] * 512 + 64 * n + s, 8, 8), :] for w, s in EDGE_COLS for n in range(8)]
    scaled, rounded = pointwise(jnp.concatenate(parts, 0), border_up[...], weights, sums)
    for e, (w, s) in enumerate(EDGE_COLS):
        for n in range(8):
            at = 384 + 64 * e + 8 * n
            nat[rows(8 * n * T + 8 * s + w, 8, T), :] = scaled[at : at + 8]
            qg[rows((8 * n + 3) * QROW + 24 + 8 * w + s, 8, QROW), :] = rounded[at : at + 8]
    for e, p in enumerate(EDGE_ROWS):
        for w in range(8):
            at = 64 * e + 8 * w
            nat[rows(p * T + w, 8, 8), :] = scaled[at : at + 8]
            qg[rows((p + 3) * QROW + 24 + 8 * w, 8), :] = rounded[at : at + 8]


def kernel_body(
    src_ref,
    sea_hbm,
    cot_hbm,
    k_ref,
    cb_ref,
    gain_ref,
    lnb_ref,
    win_ref,
    bin_ref,
    wout_ref,
    bout_ref,
    ls_ref,
    out_hbm,
    gf_hbm,
    gk_ref,
    gcb_ref,
    ggain_ref,
    glnb_ref,
    gwin_ref,
    gbin_ref,
    gwout_ref,
    gbout_ref,
    gls_ref,
    q,
    qg,
    field,
    up_field,
    border_up,
    nat,
    taps,
    corner,
    tap_acc,
    acc_win,
    acc_wout,
    acc_bin,
    acc_vec,
    frames,
    held_in,
    held_grad,
    chosen,
    halos,
    buf,
    other,
    paired,
    pieces,
    part,
    line,
    total,
    small,
    small_column,
    small_part,
    small_plane,
    small_total,
    sea_ref,
    cot_ref,
    out_ref,
    gf_ref,
    field_sems,
    ex_sent,
    ex_landed,
    sent,
    landed,
):
    t, d = lax.axis_index("tiles"), lax.axis_index("dp")
    x, zl, y = lax.div(t, 16), lax.rem(lax.div(t, 4), 4), lax.rem(t, 4)
    zh, core = lax.div(d, 2), lax.rem(d, 2)
    plane, z = 4 * x + y, 4 * zh + zl

    def in_plane(o):
        there = lax.rem(plane + o, 16)
        return there, {"tiles": 16 * lax.div(there, 4) + 4 * zl + lax.rem(there, 4), "dp": d}

    def in_line(o):
        there = lax.rem(z + o, 8)
        return there, {"tiles": 16 * x + 4 * lax.rem(there, 4) + y, "dp": 2 * lax.div(there, 4) + core}

    def in_column(o):
        there = lax.rem(2 * z + core + o, 16)
        above = lax.div(there, 2)
        return there, {
            "tiles": 16 * x + 4 * lax.rem(above, 4) + y,
            "dp": 2 * lax.div(above, 4) + lax.rem(there, 2),
        }

    def in_tiles(o):
        there = lax.rem(t + o, NT)
        return there, {"tiles": there, "dp": d}

    twin = {"tiles": t, "dp": 2 * zh + (1 - core)}

    def send(src, dst, send_sem, recv_sem, device):
        copy = pltpu.make_async_remote_copy(
            src_ref=src,
            dst_ref=dst,
            send_sem=send_sem,
            recv_sem=recv_sem,
            device_id=device,
            device_id_type=MESH,
        )
        copy.start()
        return copy

    sea_in = pltpu.make_async_copy(sea_hbm, sea_ref, field_sems.at[0])
    sea_in.start()
    cot_in = pltpu.make_async_copy(cot_hbm, cot_ref, field_sems.at[1])
    cot_in.start()

    barrier = pltpu.get_barrier_semaphore()

    def greet(device):
        pl.semaphore_signal(barrier, inc=1, device_id=device, device_id_type=MESH)

    loop(1, NT, lambda o: greet(in_tiles(o)[1]))
    for k in range(1, 4):
        loop(0, 4, lambda n, k=k: greet({"tiles": 16 * x + 4 * n + y, "dp": lax.rem(d + k, 4)}))
    held = (held_in, held_grad)

    def spread(n):
        def one(o):
            chunk, device = in_tiles(o)

            @pl.when(chunk < NCH)
            def _():
                send(frames.at[n, chunk], held[n].at[t], ex_sent.at[n, 0], ex_landed.at[n, 0], device)

        held[n][NT] = jnp.zeros((16, C), BF16)
        loop(1, NT, one)

    def hand_on(n):
        @pl.when(t < NCH)
        def _():
            held[n][t] = frames[n, t]
            wait_bytes(held[n], NT - 1, ex_landed.at[n, 0])

            def one(o):
                to, device = in_tiles(o)
                chosen[n, to] = held[n][src_ref[to]]
                send(chosen.at[n, to], halos.at[n, t], ex_sent.at[n, 1], ex_landed.at[n, 1], device)

            loop(1, NT, one)
            halos[n, t] = held[n][src_ref[t]]

    def collect(n):
        @pl.when(t < NCH)
        def _():
            wait_bytes(halos.at[n], NCH - 1, ex_landed.at[n, 1])
            wait_bytes(held[n], NCH - 1, ex_sent.at[n, 0])
            wait_bytes(held[n], NT - 1, ex_sent.at[n, 1])

        @pl.when(t >= NCH)
        def _():
            wait_bytes(halos.at[n], NCH, ex_landed.at[n, 1])
            wait_bytes(held[n], NCH, ex_sent.at[n, 0])

    def deal_input(p):
        nat[rows(aligned(p * T), T), :] = sea_ref[p].astype(F32)
        for w in range(8):
            q[rows(aligned((p + 3) * QROW + 24 + 8 * w), 8), :] = nat[rows(p * T + w, 8, 8), :]
        margins(q, p + 3)

    def no_rows(q):
        for first in (0, 67 * QROW):
            q[rows(first, 3 * QROW), :] = jnp.zeros((3 * QROW, C), F32)

    no_rows(q)
    no_rows(qg)
    sea_in.wait()
    loop(0, T, deal_input)
    pack(q, frames.at[0], corner)
    for i in range(7):
        for j in range(7):
            taps[7 * i + j] = jnp.broadcast_to(k_ref[i, pl.ds(j, 1), :], (8, C))
    pl.semaphore_wait(barrier, NT - 1 + 12)
    spread(0)

    lane = lax.broadcasted_iota(jnp.int32, (8, C), 0)

    def deal_cotangent(p):
        nat[rows(aligned(p * T), T), :] = cot_ref[p].astype(F32)
        for w in range(8):
            cells = nat[rows(p * T + w, 8, 8), :]
            if w < 3:
                cells = jnp.where(lane == 0, 0.0, cells)
            if w > 4:
                cells = jnp.where(lane == 7, 0.0, cells)
            up_field[rows(aligned(WPOS[w] * 512 + 8 * p), 8), :] = cells

    cot_in.wait()
    loop(0, T, deal_cotangent)
    for w in range(8):
        for first in (0, 61):
            up_field[rows(WPOS[w] * 512 + 8 * first, 24), :] = jnp.zeros((24, C), F32)
    for e, p in enumerate(EDGE_ROWS):
        for w in range(8):
            border_up[rows(64 * e + 8 * w, 8), :] = nat[rows(p * T + w, 8, 8), :]
    for e, (w, s) in enumerate(EDGE_COLS):
        for n in range(8):
            cells = nat[rows(8 * n * T + 8 * s + w, 8, T), :]
            if n == 0:
                cells = jnp.where(lane < 3, 0.0, cells)
            if n == 7:
                cells = jnp.where(lane > 4, 0.0, cells)
            border_up[rows(384 + 64 * e + 8 * n, 8), :] = cells
    for acc in (acc_win, acc_wout, acc_bin, acc_vec, tap_acc):
        acc[...] = jnp.zeros_like(acc)
    loop(0, 8, lambda group: convolve(q, taps, field, group, False))
    hand_on(0)

    weights = (cb_ref, gain_ref, lnb_ref, win_ref, bin_ref, wout_ref, bout_ref, ls_ref)
    sums = (acc_win, acc_wout, acc_bin, acc_vec)
    loop(0, 4, lambda b: tile_block(b, field, up_field, weights, sums, nat, qg))
    collect(0)
    neighbours_in(q, halos.at[0], corner, taps, field, False)
    border_block(field, border_up, weights, sums, nat, qg)

    for n in range(4):
        block = pl.ds(n * C, C)
        buf[block, :] = acc_win[:, block]
        buf[pl.ds(512 + n * C, C), :] = acc_wout[:, block].T
    mine = pl.multiple_of(core * HALF, HALF)
    yours = pl.multiple_of((1 - core) * HALF, HALF)
    to_twin = send(buf.at[pl.ds(yours, HALF)], other, sent.at[0], landed.at[0], twin)
    pack(qg, frames.at[1], corner)
    spread(1)
    loop(3, 3 + T, lambda row: margins(qg, row))

    def tap_rows(first, last):
        loop(first, last, lambda p: tap_sums(q, qg, tap_acc, p))

    def back_rows(first, last):
        loop(first, last, lambda group: convolve(qg, taps, field, group, True))

    to_twin.wait()
    paired[...] = (other[...] + buf[pl.ds(mine, HALF), :]).astype(BF16)

    def scatter(o):
        there, device = in_plane(o)
        at = pl.multiple_of(there * PIECE, PIECE)
        send(paired.at[pl.ds(at, PIECE)], pieces.at[plane], sent.at[1], landed.at[1], device)

    loop(1, 16, scatter)
    here = pl.multiple_of(plane * PIECE, PIECE)
    pieces[plane] = paired[pl.ds(here, PIECE), :]

    tap_rows(0, T)
    for n in range(49):
        small[rows(n, 1), :] = jnp.sum(tap_acc[n], 0, keepdims=True)
    for n in range(4):
        small[rows(49 + n, 1), :] = jnp.sum(acc_bin[:, pl.ds(n * C, C)], 0, keepdims=True)
    for n in range(5):
        small[rows(53 + n, 1), :] = jnp.sum(acc_vec[n], 0, keepdims=True)
    small[rows(58, 6), :] = jnp.zeros((6, C), F32)

    def small_scatter(o):
        there, device = in_column(o)
        at = pl.multiple_of(lax.div(there, 2) * 8, 8)
        send(small.at[pl.ds(at, 8)], small_column.at[2 * z + core], sent.at[5], landed.at[5], device)

    loop(1, 16, small_scatter)
    my_small = pl.multiple_of(z * 8, 8)
    small_column[2 * z + core] = small[pl.ds(my_small, 8), :]
    hand_on(1)

    back_rows(0, 1)

    wait_bytes(pieces, 15, landed.at[1])
    part[...] = jnp.sum(pieces[...].astype(F32), 0)
    loop(1, 8, lambda o: send(part, line.at[z], sent.at[2], landed.at[2], in_line(o)[1]) and None)
    line[z] = part[...]

    back_rows(1, 5)

    wait_bytes(small_column, 15, landed.at[5])
    small_part[...] = jnp.sum(small_column[...], 0)
    loop(
        1,
        16,
        lambda o: send(small_part, small_plane.at[plane], sent.at[7], landed.at[7], in_plane(o)[1]) and None,
    )
    small_plane[plane] = small_part[...]

    back_rows(5, 6)

    wait_bytes(line, 7, landed.at[2])
    my_piece = pl.multiple_of(mine + here, PIECE)
    total[pl.ds(my_piece, PIECE), :] = (jnp.sum(line[...], 0) * SCALE).astype(BF16)

    def gather(o):
        spot = total.at[pl.ds(my_piece, PIECE)]
        send(spot, spot, sent.at[3], landed.at[3], in_plane(o)[1])

    loop(1, 16, gather)

    back_rows(6, 8)

    wait_bytes(small_plane, 15, landed.at[7])
    small_total[pl.ds(my_small, 8), :] = jnp.sum(small_plane[...], 0) * SCALE

    def small_gather(o):
        spot = small_total.at[pl.ds(my_small, 8)]
        send(spot, spot, sent.at[8], landed.at[8], in_line(o)[1])

    loop(1, 8, small_gather)

    def write_out(p):
        at = aligned(p * T)
        out_ref[p] = (sea_ref[p].astype(F32) + nat[rows(at, T), :]).astype(BF16)

    loop(0, T, write_out)
    out_away = pltpu.make_async_copy(out_ref, out_hbm, field_sems.at[2])
    out_away.start()

    gathered = total.at[pl.ds(0, 15 * PIECE)]
    pltpu.make_async_copy(gathered, gathered, landed.at[3]).wait()
    half = total.at[pl.ds(mine, HALF)]
    last = send(half, half, sent.at[4], landed.at[4], twin)

    collect(1)
    neighbours_in(qg, halos.at[1], corner, taps, field, True)

    def write_grad(p):
        for w in range(8):
            nat[rows(p * T + w, 8, 8), :] = field[rows(aligned(WPOS[w] * 512 + 8 * p), 8), :]
        gf_ref[p] = (cot_ref[p].astype(F32) + nat[rows(aligned(p * T), T), :]).astype(BF16)

    gf_away = []
    for n in range(2):
        loop(32 * n, 32 * n + 32, write_grad)
        spot = pl.ds(32 * n, 32)
        gf_away.append(pltpu.make_async_copy(gf_ref.at[spot], gf_hbm.at[spot], field_sems.at[3 + n]))
        gf_away[n].start()

    wait_bytes(small_column, 7, landed.at[8])
    for i in range(7):
        gk_ref[i] = small_total[rows(7 * i, 7), :]
    for n in range(4):
        gbin_ref[:, pl.ds(n * C, C)] = small_total[rows(49 + n, 1), :]
    for n, ref in enumerate((gcb_ref, ggain_ref, glnb_ref, gbout_ref, gls_ref)):
        ref[...] = small_total[rows(53 + n, 1), :]
    last.wait()
    for n in range(4):
        block = pl.ds(n * C, C)
        gwin_ref[:, block] = total[block, :].astype(F32)
    gwout_ref[...] = total[pl.ds(512, 512), :].astype(F32)

    wait_bytes(pieces, 15, sent.at[1])
    wait_bytes(line, 7, sent.at[2])
    pltpu.make_async_copy(gathered, gathered, sent.at[3]).wait()
    wait_bytes(small_column, 15, sent.at[5])
    wait_bytes(small_plane, 15, sent.at[7])
    wait_bytes(small_column, 7, sent.at[8])
    for copy in (out_away, *gf_away):
        copy.wait()


def whole_block(src, sea, cot, kernel, conv_bias, ln_gain, ln_bias, w_in, b_in, w_out, b_out, layer_scale):
    vmem = pl.BlockSpec(memory_space=pltpu.VMEM)
    anywhere = pl.BlockSpec(memory_space=pl.ANY)
    vec = jax.ShapeDtypeStruct((1, C), F32)
    f32 = lambda *shape: pltpu.VMEM(shape, F32)
    bf16 = lambda *shape: pltpu.VMEM(shape, BF16)
    return pl.pallas_call(
        kernel_body,
        out_shape=(
            jax.ShapeDtypeStruct((T, T, C), BF16),
            jax.ShapeDtypeStruct((T, T, C), BF16),
            jax.ShapeDtypeStruct((7, 7, C), F32),
            vec,
            vec,
            vec,
            jax.ShapeDtypeStruct((C, HID), F32),
            jax.ShapeDtypeStruct((1, HID), F32),
            jax.ShapeDtypeStruct((HID, C), F32),
            vec,
            vec,
        ),
        in_specs=[pl.BlockSpec(memory_space=pltpu.SMEM)] + [anywhere] * 2 + [vmem] * 9,
        out_specs=(anywhere,) * 2 + (vmem,) * 9,
        scratch_shapes=[
            f32(PW * QROW, C),
            f32(PW * QROW, C),
            f32(T * T, C),
            f32(T * T, C),
            f32(BORDER, C),
            f32(T * T, C),
            f32(49, 8, C),
            f32(16, C),
            f32(49, 8, C),
            f32(C, HID),
            f32(C, HID),
            f32(8, HID),
            f32(5, 8, C),
            bf16(2, NCH, 16, C),
            bf16(NT + 1, 16, C),
            bf16(NT + 1, 16, C),
            bf16(2, NT, 16, C),
            bf16(2, NCH, 16, C),
            f32(ALL_ROWS, C),
            f32(HALF, C),
            bf16(HALF, C),
            bf16(16, PIECE, C),
            f32(PIECE, C),
            f32(8, PIECE, C),
            bf16(ALL_ROWS, C),
            f32(SMALL, C),
            f32(16, 8, C),
            f32(8, C),
            f32(16, 8, C),
            f32(SMALL, C),
            bf16(T, T, C),
            bf16(T, T, C),
            bf16(T, T, C),
            bf16(T, T, C),
            pltpu.SemaphoreType.DMA((5,)),
            pltpu.SemaphoreType.DMA((2, 2)),
            pltpu.SemaphoreType.DMA((2, 2)),
            pltpu.SemaphoreType.DMA((9,)),
            pltpu.SemaphoreType.DMA((9,)),
        ],
        compiler_params=pltpu.CompilerParams(
            collective_id=1, has_side_effects=True, vmem_limit_bytes=VMEM_LIMIT
        ),
        name="whole_block",
    )(
        src,
        sea,
        cot,
        kernel,
        conv_bias.reshape(1, C),
        ln_gain.reshape(1, C),
        ln_bias.reshape(1, C),
        w_in,
        b_in.reshape(1, HID),
        w_out,
        b_out.reshape(1, C),
        layer_scale.reshape(1, C),
    )


HAND_ROWS = 16


def hand_over_kernel(*refs):
    count = (len(refs) - 2) // 3
    here, there = refs[-2:]
    parts = []
    for n in range(count):
        a, b, mid = refs[n], refs[count + n], refs[2 * count + n]
        if a.shape[0] == T:
            for first in range(0, T, HAND_ROWS):
                parts.append([r.at[pl.ds(first, HAND_ROWS)] for r in (a, mid, b)])
        else:
            parts.append([a, mid, b])
    arrive = [pltpu.make_async_copy(a, mid, here.at[n]) for n, (a, mid, _) in enumerate(parts)]
    leave = [pltpu.make_async_copy(mid, b, there.at[n]) for n, (_, mid, b) in enumerate(parts)]
    for copy in arrive:
        copy.start()
    for first, then in zip(arrive, leave):
        first.wait()
        then.start()
    for copy in leave:
        copy.wait()


def hand_over(*arrays):
    anywhere = pl.BlockSpec(memory_space=pl.ANY)
    parts = len(arrays) + sum(T // HAND_ROWS - 1 for a in arrays if a.shape[0] == T)
    return pl.pallas_call(
        hand_over_kernel,
        out_shape=tuple(jax.ShapeDtypeStruct(a.shape, a.dtype) for a in arrays),
        in_specs=[anywhere] * len(arrays),
        out_specs=(anywhere,) * len(arrays),
        scratch_shapes=[pltpu.VMEM(a.shape, a.dtype) for a in arrays]
        + [pltpu.SemaphoreType.DMA((parts,)), pltpu.SemaphoreType.DMA((parts,))],
        name="hand_over",
    )(*arrays)


def sources(tile_deal, adjacency):
    me = lax.axis_index("tiles")
    way = jnp.where(me < 48, lax.div(me, 12), lax.rem(me, 4) + 4)
    ids = jnp.arange(NT, dtype=jnp.int32)
    picked = jnp.sum(jnp.where(jnp.arange(8)[None, :] == way, adjacency, 0), 1)
    near = jnp.sum(jnp.where(tile_deal[:, None] == ids[None, :], picked[None, :], 0), 1)
    holder = jnp.sum(jnp.where(near[:, None] == tile_deal[None, :], ids[None, :], 0), 1)
    return jnp.where(near < 0, NT, holder).astype(jnp.int32)


def on_device(
    sea_state,
    cotangent,
    kernel,
    conv_bias,
    ln_gain,
    ln_bias,
    w_in,
    b_in,
    w_out,
    b_out,
    layer_scale,
    tile_deal,
    adjacency,
):
    out, gf, gk, gcb, ggain, glnb, gwin, gbin, gwout, gbout, gls = whole_block(
        sources(tile_deal, adjacency),
        sea_state[0, 0],
        cotangent[0, 0],
        kernel,
        conv_bias,
        ln_gain,
        ln_bias,
        w_in,
        b_in,
        w_out,
        b_out,
        layer_scale,
    )
    out, gf, gk, gcb, ggain, glnb, gwin, gbin, gwout, gbout, gls = hand_over(
        out, gf, gk, gcb, ggain, glnb, gwin, gbin, gwout, gbout, gls
    )
    return (
        out[None, None],
        gf[None, None],
        gk,
        gcb.reshape(C),
        ggain.reshape(C),
        glnb.reshape(C),
        gwin,
        gbin.reshape(HID),
        gwout,
        gbout.reshape(C),
        gls.reshape(C),
    )


def solution(mesh):
    field = P("dp", "tiles", None, None, None)
    return jax.shard_map(
        on_device,
        mesh=mesh,
        in_specs=(field, field) + (P(),) * 11,
        out_specs=(field, field) + (P(),) * 9,
        check_vma=False,
    )
```

```python
import functools
import math

import jax
import jax.numpy as jnp
from jax import lax
from jax.experimental import pallas as pl
from jax.experimental.pallas import tpu as pltpu
from jax.sharding import PartitionSpec as P

MESH = pl.DeviceIdType.MESH
F32 = jnp.float32
BF16 = jnp.bfloat16

T = 64
C = 128
HID = 512
NT = 64
PW = T + 6
NCH = 52
VMEM_LIMIT = 60 * 1024 * 1024

QROW = 14 * 8
WPOS = (6, 4, 2, 0, 1, 3, 5, 7)
EDGE_ROWS = (0, 1, 2, 61, 62, 63)
EDGE_COLS = ((0, 0), (1, 0), (2, 0), (5, 7), (6, 7), (7, 7))
BORDER = 768
BLOCK = 1024

ALL_ROWS = 1024
HALF = ALL_ROWS // 2
PIECE = HALF // 16
SMALL = 64
SCALE = 1.0 / math.sqrt(4 * NT * T * T)


def rows(start, size, stride=None):
    return pl.ds(start, size) if stride is None else pl.ds(start, size, stride=stride)


def aligned(at):
    return at if isinstance(at, int) else pl.multiple_of(at, 8)


def wait_bytes(ref, count, sem):
    part = ref.at[pl.ds(0, count)]
    pltpu.make_async_copy(part, part, sem).wait()


def loop(first, last, do):
    def body(n, carry):
        do(n)
        return carry

    lax.fori_loop(first, last, body, 0)


def margins(q, row):
    base = row * QROW
    lane = lax.rem(lax.broadcasted_iota(jnp.int32, (24, C), 0), 8)
    west = q[rows(base + 24 + 39, 24), :]
    q[rows(aligned(base), 24), :] = jnp.where(lane == 0, 0.0, west)
    east = q[rows(base + 25, 24), :]
    q[rows(aligned(base + 88), 24), :] = jnp.where(lane == 7, 0.0, east)


def pack(q, frame, corner):
    for m in range(3):
        for a in range(4):
            frame[4 * m + a] = q[rows((T + m) * QROW + 24 + 16 * a, 16), :].astype(BF16)
            frame[12 + 4 * m + a] = q[rows((3 + m) * QROW + 24 + 16 * a, 16), :].astype(BF16)
    for c in range(3):
        for b in range(4):
            base = (3 + 16 * b) * QROW + 24
            frame[24 + 4 * c + b] = q[rows(base + 8 * (5 + c) + 7, 16, QROW), :].astype(BF16)
            frame[36 + 4 * c + b] = q[rows(base + 8 * c, 16, QROW), :].astype(BF16)
    corner[...] = jnp.zeros((16, C), F32)
    for n, (row, at) in enumerate(((T, 47), (T, 0), (3, 47), (3, 0))):
        for r in range(3):
            for c in range(3):
                corner[rows(4 * r + c, 1), :] = q[rows((row + r) * QROW + 24 + at + 8 * c, 1), :]
        frame[48 + n] = corner[...].astype(BF16)


def put_sides(q, halo):
    for c in range(3):
        for b in range(4):
            base = (3 + 16 * b) * QROW
            q[rows(base + 8 * c, 16, QROW), :] = halo[24 + 4 * c + b].astype(F32)
            q[rows(base + 88 + 8 * c + 7, 16, QROW), :] = halo[36 + 4 * c + b].astype(F32)


def put_ends(q, halo, corner):
    for m in range(3):
        for row, first in ((m, 0), (67 + m, 12)):
            for a in range(4):
                q[rows(row * QROW + 24 + 16 * a, 16), :] = halo[first + 4 * m + a].astype(F32)
            margins(q, row)
    for n, (row, at) in enumerate(((0, 0), (0, 95), (67, 0), (67, 95))):
        corner[...] = halo[48 + n].astype(F32)
        for r in range(3):
            for c in range(3):
                q[rows((row + r) * QROW + at + 8 * c, 1), :] = corner[rows(4 * r + c, 1), :]


def tap_at(taps, i, j, flipped):
    return taps[48 - 7 * i - j] if flipped else taps[7 * i + j]


def convolve(q, taps, field, group, flipped):
    first = group * 8
    for w in range(0, 8, 2):
        acc = [None] * 8
        for m in range(14):
            x = q[rows(aligned((first + m) * QROW + 8 * w), 64), :].reshape(8, 8, C)
            for r in range(8):
                i = m - r
                if 0 <= i < 7:
                    for j in range(7):
                        term = x[j : j + 2] * tap_at(taps, i, j, flipped)
                        acc[r] = term if acc[r] is None else acc[r] + term
        for r in range(8):
            for n in range(2):
                field[rows(aligned(WPOS[w + n] * 512 + 8 * (first + r)), 8), :] = acc[r][n]


def add_sides(q, taps, field, group, flipped):
    first = group * 8
    for side in range(2):
        acc = [None] * 3
        for i in range(7):
            for c in range(3):
                at = 8 * c if side == 0 else 88 + 8 * c + 7
                x = q[rows((first + i) * QROW + at, 8, QROW), :]
                for e in range(3):
                    j = c - e if side == 0 else 6 + c - e
                    if 0 <= j < 7:
                        term = x * tap_at(taps, i, j, flipped)
                        acc[e] = term if acc[e] is None else acc[e] + term
        for e in range(3):
            w, s = (e, 0) if side == 0 else (5 + e, 7)
            spot = rows(WPOS[w] * 512 + first * 8 + s, 8, 8)
            field[spot, :] = field[spot, :] + acc[e]


def add_ends(q, taps, field, flipped):
    for e in range(3):
        for row, inputs in ((e, range(3 - e)), (61 + e, range(6 - e, 7))):
            acc = None
            for i in inputs:
                x = q[rows((row + i) * QROW, QROW), :].reshape(14, 8, C)
                for j in range(7):
                    term = x[j : j + 8] * tap_at(taps, i, j, flipped)
                    acc = term if acc is None else acc + term
            for w in range(8):
                spot = rows(WPOS[w] * 512 + 8 * row, 8)
                field[spot, :] = field[spot, :] + acc[w]


def neighbours_in(q, halo, corner, taps, field, flipped):
    put_sides(q, halo)
    loop(0, 8, lambda group: add_sides(q, taps, field, group, flipped))
    put_ends(q, halo, corner)
    add_ends(q, taps, field, flipped)


def tap_sums(q, qg, acc, p):
    g = qg[rows(aligned((p + 3) * QROW + 24), T), :].reshape(8, 8, C)
    for i in range(7):
        x = q[rows(aligned((p + i) * QROW), QROW), :].reshape(14, 8, C)
        for j in range(7):
            acc[7 * i + j] += jnp.sum(x[j : j + 8] * g, 0)


def fold(x):
    return jnp.sum(x.reshape(x.shape[0] // 8, 8, x.shape[1]), 0)


def dot(a, b, contract):
    return lax.dot_general(a, b, (contract, ((), ())), preferred_element_type=F32)


def pointwise(convolved, up, weights, sums):
    cb_ref, gain_ref, lnb_ref, win_ref, bin_ref, wout_ref, bout_ref, ls_ref = weights
    acc_win, acc_wout, acc_bin, acc_vec = sums
    convolved = convolved + cb_ref[...]
    centred = convolved - jnp.mean(convolved, -1, keepdims=True)
    inv_std = lax.rsqrt(jnp.mean(centred * centred, -1, keepdims=True) + 1e-06)
    whitened = centred * inv_std
    normed = (whitened * gain_ref[...] + lnb_ref[...]).astype(BF16)
    grad_out = up * ls_ref[...]
    grad_out16 = grad_out.astype(BF16)
    c0 = math.sqrt(2 / math.pi)
    c1 = c0 * 0.044715
    v = dot(normed, win_ref[...], ((1,), (0,))) + bin_ref[...]
    v2 = v * v
    t = jnp.tanh(v * (c0 + c1 * v2))
    half = 0.5 + 0.5 * t
    act = v * half
    slope = half + act * (1.0 - t) * (c0 + (3 * c1) * v2)
    act16 = act.astype(BF16)
    branch = bout_ref[...] + dot(act16, wout_ref[...], ((1,), (0,)))
    acc_wout[...] += dot(grad_out16, act16, ((0,), (0,)))
    grad_pre = slope * dot(grad_out16, wout_ref[...], ((1,), (1,)))
    grad_pre16 = grad_pre.astype(BF16)
    acc_bin[...] += fold(grad_pre)
    acc_win[...] += dot(normed, grad_pre16, ((0,), (0,)))
    grad_normed = dot(grad_pre16, win_ref[...], ((1,), (1,)))
    grad_white = grad_normed * gain_ref[...]
    grad_conv = inv_std * (
        grad_white
        - jnp.mean(grad_white, -1, keepdims=True)
        - whitened * jnp.mean(grad_white * whitened, -1, keepdims=True)
    )
    acc_vec[0] += fold(grad_conv)
    acc_vec[1] += fold(grad_normed * whitened)
    acc_vec[2] += fold(grad_normed)
    acc_vec[3] += fold(grad_out)
    acc_vec[4] += fold(up * branch)
    return branch * ls_ref[...], grad_conv.astype(BF16).astype(F32)


def tile_block(b, field, up_field, weights, sums, nat, qg):
    spot = rows(pl.multiple_of(b * BLOCK, BLOCK), BLOCK)
    scaled, rounded = pointwise(field[spot, :], up_field[spot, :], weights, sums)
    for n, w in enumerate((3 - b, 4 + b)):
        for p in range(T):
            at = 512 * n + 8 * p
            nat[rows(p * T + w, 8, 8), :] = scaled[at : at + 8]
            qg[rows(aligned((p + 3) * QROW + 24 + 8 * w), 8), :] = rounded[at : at + 8]


def border_block(field, border_up, weights, sums, nat, qg):
    parts = [field[rows(WPOS[w] * 512 + 8 * p, 8), :] for p in EDGE_ROWS for w in range(8)]
    parts += [field[rows(WPOS[w] * 512 + 64 * n + s, 8, 8), :] for w, s in EDGE_COLS for n in range(8)]
    scaled, rounded = pointwise(jnp.concatenate(parts, 0), border_up[...], weights, sums)
    for e, (w, s) in enumerate(EDGE_COLS):
        for n in range(8):
            at = 384 + 64 * e + 8 * n
            nat[rows(8 * n * T + 8 * s + w, 8, T), :] = scaled[at : at + 8]
            qg[rows((8 * n + 3) * QROW + 24 + 8 * w + s, 8, QROW), :] = rounded[at : at + 8]
    for e, p in enumerate(EDGE_ROWS):
        for w in range(8):
            at = 64 * e + 8 * w
            nat[rows(p * T + w, 8, 8), :] = scaled[at : at + 8]
            qg[rows((p + 3) * QROW + 24 + 8 * w, 8), :] = rounded[at : at + 8]


def kernel_body(
    src_ref,
    sea_hbm,
    cot_hbm,
    k_ref,
    cb_ref,
    gain_ref,
    lnb_ref,
    win_ref,
    bin_ref,
    wout_ref,
    bout_ref,
    ls_ref,
    out_hbm,
    gf_hbm,
    gk_ref,
    gcb_ref,
    ggain_ref,
    glnb_ref,
    gwin_ref,
    gbin_ref,
    gwout_ref,
    gbout_ref,
    gls_ref,
    q,
    qg,
    field,
    up_field,
    border_up,
    nat,
    taps,
    corner,
    tap_acc,
    acc_win,
    acc_wout,
    acc_bin,
    acc_vec,
    frames,
    held_in,
    held_grad,
    chosen,
    halos,
    buf,
    other,
    paired,
    pieces,
    part,
    line,
    total,
    small,
    small_column,
    small_part,
    small_plane,
    small_total,
    sea_ref,
    cot_ref,
    out_ref,
    gf_ref,
    field_sems,
    ex_sent,
    ex_landed,
    sent,
    landed,
):
    t, d = lax.axis_index("tiles"), lax.axis_index("dp")
    x, zl, y = lax.div(t, 16), lax.rem(lax.div(t, 4), 4), lax.rem(t, 4)
    zh, core = lax.div(d, 2), lax.rem(d, 2)
    plane, z = 4 * x + y, 4 * zh + zl

    def in_plane(o):
        there = lax.rem(plane + o, 16)
        return there, {"tiles": 16 * lax.div(there, 4) + 4 * zl + lax.rem(there, 4), "dp": d}

    def in_line(o):
        there = lax.rem(z + o, 8)
        return there, {"tiles": 16 * x + 4 * lax.rem(there, 4) + y, "dp": 2 * lax.div(there, 4) + core}

    def in_column(o):
        there = lax.rem(2 * z + core + o, 16)
        above = lax.div(there, 2)
        return there, {
            "tiles": 16 * x + 4 * lax.rem(above, 4) + y,
            "dp": 2 * lax.div(above, 4) + lax.rem(there, 2),
        }

    def in_tiles(o):
        there = lax.rem(t + o, NT)
        return there, {"tiles": there, "dp": d}

    twin = {"tiles": t, "dp": 2 * zh + (1 - core)}

    def send(src, dst, send_sem, recv_sem, device):
        copy = pltpu.make_async_remote_copy(
            src_ref=src,
            dst_ref=dst,
            send_sem=send_sem,
            recv_sem=recv_sem,
            device_id=device,
            device_id_type=MESH,
        )
        copy.start()
        return copy

    sea_in = pltpu.make_async_copy(sea_hbm, sea_ref, field_sems.at[0])
    sea_in.start()
    cot_in = pltpu.make_async_copy(cot_hbm, cot_ref, field_sems.at[1])
    cot_in.start()

    barrier = pltpu.get_barrier_semaphore()

    def greet(device):
        pl.semaphore_signal(barrier, inc=1, device_id=device, device_id_type=MESH)

    loop(1, NT, lambda o: greet(in_tiles(o)[1]))
    for k in range(1, 4):
        loop(0, 4, lambda n, k=k: greet({"tiles": 16 * x + 4 * n + y, "dp": lax.rem(d + k, 4)}))
    held = (held_in, held_grad)

    def spread(n):
        def one(o):
            chunk, device = in_tiles(o)

            @pl.when(chunk < NCH)
            def _():
                send(frames.at[n, chunk], held[n].at[t], ex_sent.at[n, 0], ex_landed.at[n, 0], device)

        held[n][NT] = jnp.zeros((16, C), BF16)
        loop(1, NT, one)

    def hand_on(n):
        @pl.when(t < NCH)
        def _():
            held[n][t] = frames[n, t]
            wait_bytes(held[n], NT - 1, ex_landed.at[n, 0])

            def one(o):
                to, device = in_tiles(o)
                chosen[n, to] = held[n][src_ref[to]]
                send(chosen.at[n, to], halos.at[n, t], ex_sent.at[n, 1], ex_landed.at[n, 1], device)

            loop(1, NT, one)
            halos[n, t] = held[n][src_ref[t]]

    def collect(n):
        @pl.when(t < NCH)
        def _():
            wait_bytes(halos.at[n], NCH - 1, ex_landed.at[n, 1])
            wait_bytes(held[n], NCH - 1, ex_sent.at[n, 0])
            wait_bytes(held[n], NT - 1, ex_sent.at[n, 1])

        @pl.when(t >= NCH)
        def _():
            wait_bytes(halos.at[n], NCH, ex_landed.at[n, 1])
            wait_bytes(held[n], NCH, ex_sent.at[n, 0])

    def deal_input(p):
        nat[rows(aligned(p * T), T), :] = sea_ref[p].astype(F32)
        for w in range(8):
            q[rows(aligned((p + 3) * QROW + 24 + 8 * w), 8), :] = nat[rows(p * T + w, 8, 8), :]
        margins(q, p + 3)

    def no_rows(q):
        for first in (0, 67 * QROW):
            q[rows(first, 3 * QROW), :] = jnp.zeros((3 * QROW, C), F32)

    no_rows(q)
    no_rows(qg)
    sea_in.wait()
    loop(0, T, deal_input)
    pack(q, frames.at[0], corner)
    for i in range(7):
        for j in range(7):
            taps[7 * i + j] = jnp.broadcast_to(k_ref[i, pl.ds(j, 1), :], (8, C))
    pl.semaphore_wait(barrier, NT - 1 + 12)
    spread(0)

    lane = lax.broadcasted_iota(jnp.int32, (8, C), 0)

    def deal_cotangent(p):
        nat[rows(aligned(p * T), T), :] = cot_ref[p].astype(F32)
        for w in range(8):
            cells = nat[rows(p * T + w, 8, 8), :]
            if w < 3:
                cells = jnp.where(lane == 0, 0.0, cells)
            if w > 4:
                cells = jnp.where(lane == 7, 0.0, cells)
            up_field[rows(aligned(WPOS[w] * 512 + 8 * p), 8), :] = cells

    cot_in.wait()
    loop(0, T, deal_cotangent)
    for w in range(8):
        for first in (0, 61):
            up_field[rows(WPOS[w] * 512 + 8 * first, 24), :] = jnp.zeros((24, C), F32)
    for e, p in enumerate(EDGE_ROWS):
        for w in range(8):
            border_up[rows(64 * e + 8 * w, 8), :] = nat[rows(p * T + w, 8, 8), :]
    for e, (w, s) in enumerate(EDGE_COLS):
        for n in range(8):
            cells = nat[rows(8 * n * T + 8 * s + w, 8, T), :]
            if n == 0:
                cells = jnp.where(lane < 3, 0.0, cells)
            if n == 7:
                cells = jnp.where(lane > 4, 0.0, cells)
            border_up[rows(384 + 64 * e + 8 * n, 8), :] = cells
    for acc in (acc_win, acc_wout, acc_bin, acc_vec, tap_acc):
        acc[...] = jnp.zeros_like(acc)
    loop(0, 8, lambda group: convolve(q, taps, field, group, False))
    hand_on(0)

    weights = (cb_ref, gain_ref, lnb_ref, win_ref, bin_ref, wout_ref, bout_ref, ls_ref)
    sums = (acc_win, acc_wout, acc_bin, acc_vec)
    loop(0, 4, lambda b: tile_block(b, field, up_field, weights, sums, nat, qg))
    collect(0)
    neighbours_in(q, halos.at[0], corner, taps, field, False)
    border_block(field, border_up, weights, sums, nat, qg)

    for n in range(4):
        block = pl.ds(n * C, C)
        buf[block, :] = acc_win[:, block]
        buf[pl.ds(512 + n * C, C), :] = acc_wout[:, block].T
    mine = pl.multiple_of(core * HALF, HALF)
    yours = pl.multiple_of((1 - core) * HALF, HALF)
    to_twin = send(buf.at[pl.ds(yours, HALF)], other, sent.at[0], landed.at[0], twin)
    pack(qg, frames.at[1], corner)
    spread(1)
    loop(3, 3 + T, lambda row: margins(qg, row))

    def tap_rows(first, last):
        loop(first, last, lambda p: tap_sums(q, qg, tap_acc, p))

    def back_rows(first, last):
        loop(first, last, lambda group: convolve(qg, taps, field, group, True))

    to_twin.wait()
    paired[...] = (other[...] + buf[pl.ds(mine, HALF), :]).astype(BF16)

    def scatter(o):
        there, device = in_plane(o)
        at = pl.multiple_of(there * PIECE, PIECE)
        send(paired.at[pl.ds(at, PIECE)], pieces.at[plane], sent.at[1], landed.at[1], device)

    loop(1, 16, scatter)
    here = pl.multiple_of(plane * PIECE, PIECE)
    pieces[plane] = paired[pl.ds(here, PIECE), :]

    tap_rows(0, 48)

    wait_bytes(pieces, 15, landed.at[1])
    part[...] = jnp.sum(pieces[...].astype(F32), 0)
    loop(1, 8, lambda o: send(part, line.at[z], sent.at[2], landed.at[2], in_line(o)[1]) and None)
    line[z] = part[...]

    tap_rows(48, T)
    for n in range(49):
        small[rows(n, 1), :] = jnp.sum(tap_acc[n], 0, keepdims=True)
    for n in range(4):
        small[rows(49 + n, 1), :] = jnp.sum(acc_bin[:, pl.ds(n * C, C)], 0, keepdims=True)
    for n in range(5):
        small[rows(53 + n, 1), :] = jnp.sum(acc_vec[n], 0, keepdims=True)
    small[rows(58, 6), :] = jnp.zeros((6, C), F32)

    def small_scatter(o):
        there, device = in_column(o)
        at = pl.multiple_of(lax.div(there, 2) * 8, 8)
        send(small.at[pl.ds(at, 8)], small_column.at[2 * z + core], sent.at[5], landed.at[5], device)

    loop(1, 16, small_scatter)
    my_small = pl.multiple_of(z * 8, 8)
    small_column[2 * z + core] = small[pl.ds(my_small, 8), :]
    hand_on(1)

    back_rows(0, 3)

    wait_bytes(small_column, 15, landed.at[5])
    small_part[...] = jnp.sum(small_column[...], 0)
    loop(
        1,
        16,
        lambda o: send(small_part, small_plane.at[plane], sent.at[7], landed.at[7], in_plane(o)[1]) and None,
    )
    small_plane[plane] = small_part[...]

    wait_bytes(line, 7, landed.at[2])
    my_piece = pl.multiple_of(mine + here, PIECE)
    total[pl.ds(my_piece, PIECE), :] = (jnp.sum(line[...], 0) * SCALE).astype(BF16)

    def gather(o):
        spot = total.at[pl.ds(my_piece, PIECE)]
        send(spot, spot, sent.at[3], landed.at[3], in_plane(o)[1])

    loop(1, 16, gather)

    back_rows(3, 8)

    wait_bytes(small_plane, 15, landed.at[7])
    small_total[pl.ds(my_small, 8), :] = jnp.sum(small_plane[...], 0) * SCALE

    def small_gather(o):
        spot = small_total.at[pl.ds(my_small, 8)]
        send(spot, spot, sent.at[8], landed.at[8], in_line(o)[1])

    loop(1, 8, small_gather)

    gathered = total.at[pl.ds(0, 15 * PIECE)]
    pltpu.make_async_copy(gathered, gathered, landed.at[3]).wait()
    half = total.at[pl.ds(mine, HALF)]
    last = send(half, half, sent.at[4], landed.at[4], twin)

    def write_out(p):
        at = aligned(p * T)
        out_ref[p] = (sea_ref[p].astype(F32) + nat[rows(at, T), :]).astype(BF16)

    loop(0, T, write_out)
    out_away = pltpu.make_async_copy(out_ref, out_hbm, field_sems.at[2])
    out_away.start()

    collect(1)
    neighbours_in(qg, halos.at[1], corner, taps, field, True)

    def write_grad(p):
        for w in range(8):
            nat[rows(p * T + w, 8, 8), :] = field[rows(aligned(WPOS[w] * 512 + 8 * p), 8), :]
        gf_ref[p] = (cot_ref[p].astype(F32) + nat[rows(aligned(p * T), T), :]).astype(BF16)

    gf_away = []
    for n in range(2):
        loop(32 * n, 32 * n + 32, write_grad)
        spot = pl.ds(32 * n, 32)
        gf_away.append(pltpu.make_async_copy(gf_ref.at[spot], gf_hbm.at[spot], field_sems.at[3 + n]))
        gf_away[n].start()

    wait_bytes(small_column, 7, landed.at[8])
    for i in range(7):
        gk_ref[i] = small_total[rows(7 * i, 7), :]
    for n in range(4):
        gbin_ref[:, pl.ds(n * C, C)] = small_total[rows(49 + n, 1), :]
    for n, ref in enumerate((gcb_ref, ggain_ref, glnb_ref, gbout_ref, gls_ref)):
        ref[...] = small_total[rows(53 + n, 1), :]
    last.wait()
    for n in range(4):
        block = pl.ds(n * C, C)
        gwin_ref[:, block] = total[block, :].astype(F32)
    gwout_ref[...] = total[pl.ds(512, 512), :].astype(F32)

    wait_bytes(pieces, 15, sent.at[1])
    wait_bytes(line, 7, sent.at[2])
    pltpu.make_async_copy(gathered, gathered, sent.at[3]).wait()
    wait_bytes(small_column, 15, sent.at[5])
    wait_bytes(small_plane, 15, sent.at[7])
    wait_bytes(small_column, 7, sent.at[8])
    for copy in (out_away, *gf_away):
        copy.wait()


def whole_block(src, sea, cot, kernel, conv_bias, ln_gain, ln_bias, w_in, b_in, w_out, b_out, layer_scale):
    vmem = pl.BlockSpec(memory_space=pltpu.VMEM)
    anywhere = pl.BlockSpec(memory_space=pl.ANY)
    vec = jax.ShapeDtypeStruct((1, C), F32)
    f32 = lambda *shape: pltpu.VMEM(shape, F32)
    bf16 = lambda *shape: pltpu.VMEM(shape, BF16)
    return pl.pallas_call(
        kernel_body,
        out_shape=(
            jax.ShapeDtypeStruct((T, T, C), BF16),
            jax.ShapeDtypeStruct((T, T, C), BF16),
            jax.ShapeDtypeStruct((7, 7, C), F32),
            vec,
            vec,
            vec,
            jax.ShapeDtypeStruct((C, HID), F32),
            jax.ShapeDtypeStruct((1, HID), F32),
            jax.ShapeDtypeStruct((HID, C), F32),
            vec,
            vec,
        ),
        in_specs=[pl.BlockSpec(memory_space=pltpu.SMEM)] + [anywhere] * 2 + [vmem] * 9,
        out_specs=(anywhere,) * 2 + (vmem,) * 9,
        scratch_shapes=[
            f32(PW * QROW, C),
            f32(PW * QROW, C),
            f32(T * T, C),
            f32(T * T, C),
            f32(BORDER, C),
            f32(T * T, C),
            f32(49, 8, C),
            f32(16, C),
            f32(49, 8, C),
            f32(C, HID),
            f32(C, HID),
            f32(8, HID),
            f32(5, 8, C),
            bf16(2, NCH, 16, C),
            bf16(NT + 1, 16, C),
            bf16(NT + 1, 16, C),
            bf16(2, NT, 16, C),
            bf16(2, NCH, 16, C),
            f32(ALL_ROWS, C),
            f32(HALF, C),
            bf16(HALF, C),
            bf16(16, PIECE, C),
            f32(PIECE, C),
            f32(8, PIECE, C),
            bf16(ALL_ROWS, C),
            f32(SMALL, C),
            f32(16, 8, C),
            f32(8, C),
            f32(16, 8, C),
            f32(SMALL, C),
            bf16(T, T, C),
            bf16(T, T, C),
            bf16(T, T, C),
            bf16(T, T, C),
            pltpu.SemaphoreType.DMA((5,)),
            pltpu.SemaphoreType.DMA((2, 2)),
            pltpu.SemaphoreType.DMA((2, 2)),
            pltpu.SemaphoreType.DMA((9,)),
            pltpu.SemaphoreType.DMA((9,)),
        ],
        compiler_params=pltpu.CompilerParams(
            collective_id=1, has_side_effects=True, vmem_limit_bytes=VMEM_LIMIT
        ),
        name="whole_block",
    )(
        src,
        sea,
        cot,
        kernel,
        conv_bias.reshape(1, C),
        ln_gain.reshape(1, C),
        ln_bias.reshape(1, C),
        w_in,
        b_in.reshape(1, HID),
        w_out,
        b_out.reshape(1, C),
        layer_scale.reshape(1, C),
    )


HAND_ROWS = 16


def hand_over_kernel(*refs):
    count = (len(refs) - 2) // 3
    here, there = refs[-2:]
    parts = []
    for n in range(count):
        a, b, mid = refs[n], refs[count + n], refs[2 * count + n]
        if a.shape[0] == T:
            for first in range(0, T, HAND_ROWS):
                parts.append([r.at[pl.ds(first, HAND_ROWS)] for r in (a, mid, b)])
        else:
            parts.append([a, mid, b])
    arrive = [pltpu.make_async_copy(a, mid, here.at[n]) for n, (a, mid, _) in enumerate(parts)]
    leave = [pltpu.make_async_copy(mid, b, there.at[n]) for n, (_, mid, b) in enumerate(parts)]
    for copy in arrive:
        copy.start()
    for first, then in zip(arrive, leave):
        first.wait()
        then.start()
    for copy in leave:
        copy.wait()


def hand_over(*arrays):
    anywhere = pl.BlockSpec(memory_space=pl.ANY)
    parts = len(arrays) + sum(T // HAND_ROWS - 1 for a in arrays if a.shape[0] == T)
    return pl.pallas_call(
        hand_over_kernel,
        out_shape=tuple(jax.ShapeDtypeStruct(a.shape, a.dtype) for a in arrays),
        in_specs=[anywhere] * len(arrays),
        out_specs=(anywhere,) * len(arrays),
        scratch_shapes=[pltpu.VMEM(a.shape, a.dtype) for a in arrays]
        + [pltpu.SemaphoreType.DMA((parts,)), pltpu.SemaphoreType.DMA((parts,))],
        name="hand_over",
    )(*arrays)


def sources(tile_deal, adjacency):
    me = lax.axis_index("tiles")
    way = jnp.where(me < 48, lax.div(me, 12), lax.rem(me, 4) + 4)
    ids = jnp.arange(NT, dtype=jnp.int32)
    picked = jnp.sum(jnp.where(jnp.arange(8)[None, :] == way, adjacency, 0), 1)
    near = jnp.sum(jnp.where(tile_deal[:, None] == ids[None, :], picked[None, :], 0), 1)
    holder = jnp.sum(jnp.where(near[:, None] == tile_deal[None, :], ids[None, :], 0), 1)
    return jnp.where(near < 0, NT, holder).astype(jnp.int32)


def on_device(
    sea_state,
    cotangent,
    kernel,
    conv_bias,
    ln_gain,
    ln_bias,
    w_in,
    b_in,
    w_out,
    b_out,
    layer_scale,
    tile_deal,
    adjacency,
):
    out, gf, gk, gcb, ggain, glnb, gwin, gbin, gwout, gbout, gls = whole_block(
        sources(tile_deal, adjacency),
        sea_state[0, 0],
        cotangent[0, 0],
        kernel,
        conv_bias,
        ln_gain,
        ln_bias,
        w_in,
        b_in,
        w_out,
        b_out,
        layer_scale,
    )
    out, gf, gk, gcb, ggain, glnb, gwin, gbin, gwout, gbout, gls = hand_over(
        out, gf, gk, gcb, ggain, glnb, gwin, gbin, gwout, gbout, gls
    )
    return (
        out[None, None],
        gf[None, None],
        gk,
        gcb.reshape(C),
        ggain.reshape(C),
        glnb.reshape(C),
        gwin,
        gbin.reshape(HID),
        gwout,
        gbout.reshape(C),
        gls.reshape(C),
    )


def solution(mesh):
    field = P("dp", "tiles", None, None, None)
    return jax.shard_map(
        on_device,
        mesh=mesh,
        in_specs=(field, field) + (P(),) * 11,
        out_specs=(field, field) + (P(),) * 9,
        check_vma=False,
    )
```
